256 devices in a mesh: cable: 64 (over z_lo, y, x), freq: 4 (over z_hi, core).
Axes of the slice: x: 4, y: 4, z: 8 (z_hi: 2, z_lo: 4; z = z_hi * 4 + z_lo), core: 2. Of those that a mesh axis runs over, the one named last changes fastest.
Arguments:
- spectra: bfloat16 [2, 24576, 512], P(None, 'cable', 'freq'), may hold values from -6 to 6
- slow_bins: int32 [192, 16384], P(None, 'cable'), may hold values from 0 to 199
- weight_steps: int32 [192, 16384], P(None, 'cable'), may hold values from 0 to 64
- delays: int32 [192, 16384], P(None, 'cable'), may hold values from 0 to 1999
Outputs:
- node_spectra: float32 [16384, 2, 512], P('cable', None, 'freq')
- beam_power: float32 [16384], P('cable')
The draws below stay inside these ranges and needn't reach their ends.
Inputs may be any that keep to these rules, and one draw needn't show every extreme that they name: `slow_bins`: the bin and the bin above it are both slownesses.
All inputs are finite; a program needn't handle non-finite values.
Results may differ from the reference program's by a relative error of at most 0.0035.
Values may be sent and summed in bfloat16 or wider, within the bound.
A program may use at most 192 MiB of HBM per device.

```python
import math
import jax
import jax.numpy as jnp
from jax import lax

NODE_DEV = 256
SUB_LEN = 256
SLOW = 201
NT = 2000
BIN0 = 20
WSTEPS = 64
SUBARRAYS = 192
CHANNELS = 24576
NFREQ = 512
NODES = 16384


def plant(values, own_key, least, top_value):
    place = [jax.random.randint(jax.random.fold_in(own_key, axis), (), 0, length) for axis, length in enumerate(values.shape)]
    main_axis = values.shape.index(max(values.shape))
    beside = place[:main_axis] + [(place[main_axis] + 1) % values.shape[main_axis]] + place[main_axis + 1:]
    return values.at[tuple(place)].set(least).at[tuple(beside)].set(top_value)


def steps_of(key, extent, split, least, largest):
    def one(axis_at, shards_of):
        steps = jax.random.uniform(jax.random.fold_in(jax.random.fold_in(key, 6), axis_at), (shards_of,), jnp.float32, least / len(split), largest / len(split))
        return jnp.repeat(jnp.exp(steps), extent[axis_at] // shards_of).reshape((-1,) + (1,) * (len(extent) - axis_at - 1))

    loudness = one(*split[0])
    for cut in split[1:]:
        loudness = loudness * one(*cut)
    return loudness


def scatter_about(rng, extent, width, most, pieces=(), kind=jnp.bfloat16):
    loudness = steps_of(rng, extent, pieces, -0.22, 0.18) if pieces else 1.0
    values = jax.random.normal(rng, extent, jnp.float32) * width * loudness
    return jnp.minimum(jnp.maximum(values, -most), most).astype(kind)


def setup_inputs(seed: int = 0) -> dict:
    key_of = jax.random.split(jax.random.key(seed), 5)
    spectra = scatter_about(key_of[0], (2, CHANNELS, NFREQ), 1.0, 6.0, ((1, 64), (2, 4)))
    slow_bins = plant(jax.random.randint(key_of[1], (SUBARRAYS, NODES), 0, SLOW - 1), jax.random.fold_in(key_of[1], 1), 0, (SLOW - 1) - 1).astype(jnp.int32)
    weight_steps = plant(jax.random.randint(key_of[2], (SUBARRAYS, NODES), 0, WSTEPS + 1), jax.random.fold_in(key_of[2], 1), 0, WSTEPS).astype(jnp.int32)
    delays = plant(jax.random.randint(key_of[3], (SUBARRAYS, NODES), 0, NT), jax.random.fold_in(key_of[3], 1), 0, NT - 1).astype(jnp.int32)
    return {"spectra": spectra, "slow_bins": slow_bins, "weight_steps": weight_steps, "delays": delays}


def steering_table(freq_bins):
    offsets = jnp.arange(SUB_LEN, dtype=jnp.int32)
    slowness = jnp.arange(SLOW, dtype=jnp.int32) - SLOW // 2
    product = freq_bins[:, None, None] * offsets[None, :, None] * slowness[None, None, :]
    modulus = 50 * NT
    angles = jnp.mod(product, modulus).astype(jnp.float32) * (2.0 * math.pi / modulus)
    factor = SUB_LEN ** -0.5
    cosine = jnp.cos(angles) * factor
    sine = jnp.sin(angles) * factor
    upper_rows = jnp.concatenate([cosine, -sine], axis=2)
    lower_rows = jnp.concatenate([sine, cosine], axis=2)
    return jnp.concatenate([upper_rows, lower_rows], axis=1).astype(jnp.bfloat16)


def subarray_frames(extended, stride_len):
    channel_len = extended.shape[1] - stride_len
    sub_count = channel_len // stride_len
    freq_len = extended.shape[2]
    first_half = extended[:, :channel_len].reshape(2, sub_count, stride_len, freq_len)
    second_half = extended[:, stride_len:].reshape(2, sub_count, stride_len, freq_len)
    frames = jnp.concatenate([first_half, second_half], axis=2)
    return jnp.transpose(frames, (1, 0, 2, 3)).reshape(sub_count, 2 * SUB_LEN, freq_len)


def slant_stack(frames, freq_bins):
    sub_count, row_len, freq_len = frames.shape
    block_len = min(16, freq_len)
    num_blocks = freq_len // block_len
    blocked = jnp.transpose(frames.reshape(sub_count, row_len, num_blocks, block_len), (2, 0, 1, 3))
    bins_blocked = freq_bins.reshape(num_blocks, block_len)

    def one_block(operands):
        frame_block, bin_block = operands
        weights = steering_table(bin_block)
        stacked = jnp.einsum("amf,fmq->faq", frame_block.astype(jnp.float32), weights.astype(jnp.float32), precision=lax.Precision.HIGHEST)
        stacked = stacked.astype(jnp.bfloat16).reshape(block_len, sub_count, 2, SLOW)
        return jnp.transpose(stacked, (1, 3, 2, 0))

    result = lax.map(one_block, (blocked, bins_blocked))
    return jnp.transpose(result, (1, 2, 3, 0, 4)).reshape(sub_count, SLOW, 2, freq_len)


def project_nodes(beam_table, bin_table, step_table, delay_table, freq_bins):
    def pick_rows(table_slab, index_row):
        return table_slab[index_row]

    lower_beam = jax.vmap(pick_rows)(beam_table, bin_table).astype(jnp.float32)
    upper_beam = jax.vmap(pick_rows)(beam_table, bin_table + 1).astype(jnp.float32)
    fraction = (step_table.astype(jnp.float32) / WSTEPS)[:, :, None, None]
    value = lower_beam + fraction * (upper_beam - lower_beam)
    phase_index = jnp.mod(delay_table[:, :, None] * freq_bins[None, None, :], NT)
    phase = phase_index.astype(jnp.float32) * (2.0 * math.pi / NT)
    cosine = jnp.cos(phase)
    sine = jnp.sin(phase)
    real_part = value[:, :, 0] * cosine - value[:, :, 1] * sine
    imag_part = value[:, :, 0] * sine + value[:, :, 1] * cosine
    return jnp.stack([jnp.sum(real_part, axis=0), jnp.sum(imag_part, axis=0)], axis=1)


def reference(spectra, slow_bins, weight_steps, delays):
    stride_len = SUB_LEN // 2
    freq_bins = BIN0 + jnp.arange(NFREQ, dtype=jnp.int32)
    extended = jnp.concatenate([spectra, jnp.zeros((2, stride_len, NFREQ), spectra.dtype)], axis=1)
    beam_table = slant_stack(subarray_frames(extended, stride_len), freq_bins)
    group_count = NODES // NODE_DEV

    def by_groups(table):
        return jnp.transpose(table.reshape(SUBARRAYS, group_count, NODE_DEV), (1, 0, 2))

    def node_group(operands):
        bin_table, step_table, delay_table = operands
        return project_nodes(beam_table, bin_table, step_table, delay_table, freq_bins)

    grouped = lax.map(node_group, (by_groups(slow_bins), by_groups(weight_steps), by_groups(delays)))
    node_spectra = grouped.reshape(NODES, 2, NFREQ) * (SUBARRAYS ** -0.5)
    beam_power = jnp.sum(node_spectra * node_spectra, axis=(1, 2)) / NFREQ
    return node_spectra, beam_power
```

```python
import functools
import math

import jax
import jax.numpy as jnp
import numpy as np
from jax import lax
from jax.experimental import pallas as pl
from jax.experimental.pallas import tpu as pltpu
from jax.sharding import PartitionSpec as P

SUB_LEN = 256
SLOW = 201
NT = 2000
BIN0 = 20
WSTEPS = 64
HALF = SLOW // 2
STRIDE = SUB_LEN // 2

Z, Y, X = 4, 4, 4
PLANE = Y * X
FREQ_DEV = 4
F = 128
N = 256
BLOCKS = 3
SHARD = BLOCKS * 2 * F
LOCAL = BLOCKS * PLANE
ROWS = LOCAL + 1
PAD_ROWS = 56
FT = F // 8
GROUP = 7
MESH = pl.DeviceIdType.MESH


def power_series(fun, degree):
    fit = np.polynomial.chebyshev.Chebyshev.interpolate(fun, degree, domain=[0.0, 0.25])
    return [float(c) for c in fit.convert(kind=np.polynomial.Polynomial, domain=[-1, 1], window=[-1, 1]).coef]


COS_TERMS = power_series(lambda v: np.cos(2 * np.pi * np.sqrt(v)), 7)
SIN_TERMS = power_series(lambda v: 2 * np.pi * np.sinc(2 * np.sqrt(v)), 6)


def horner(v, terms):
    total = jnp.full_like(v, terms[-1])
    for term in terms[-2::-1]:
        total = total * v + term
    return total


def unit_circle(count, period):
    rest = count - jnp.round(count * (1.0 / period)) * period
    turns = rest * (1.0 / period)
    v = turns * turns
    return horner(v, COS_TERMS), horner(v, SIN_TERMS) * turns


def places():
    cable = lax.axis_index("cable")
    z = cable // PLANE
    y = (cable // X) % Y
    x = cable % X
    return z, y, x


def cable_id(z, y, x):
    return {"cable": (z * Y + y) * X + x}


def steering(f, first_bin, table):
    period = float(50 * NT)
    bins = (first_bin + f).astype(jnp.float32)
    k = lax.broadcasted_iota(jnp.int32, (8, 128), 0).astype(jnp.float32)
    s = lax.broadcasted_iota(jnp.int32, (8, 128), 1).astype(jnp.float32)
    bs = s * bins
    cos0, sin0 = unit_circle(bs * k, period)
    cos8, sin8 = unit_circle(bs * 8.0, period)
    factor = SUB_LEN ** -0.5
    cos0, sin0 = cos0 * factor, sin0 * factor
    cos1, sin1 = cos0 * cos8 - sin0 * sin8, sin0 * cos8 + cos0 * sin8
    twice = cos8 + cos8
    for step in range(SUB_LEN // 16):
        rows = pl.ds(step * 16, 16)
        table[f, rows, 0:128] = jnp.concatenate([cos0, cos1], axis=0).astype(jnp.bfloat16)
        table[f, rows, 128:256] = jnp.concatenate([sin0, sin1], axis=0).astype(jnp.bfloat16)
        cos0, sin0 = twice * cos1 - cos0, twice * sin1 - sin0
        cos1, sin1 = twice * cos0 - cos1, twice * sin0 - sin1


def widen(gathered, wide):
    per = 2 * F
    wide[0:per] = jnp.zeros((per, 128), jnp.float32)
    wide[(LOCAL + 1) * per:(LOCAL + 2) * per] = jnp.zeros((per, 128), jnp.float32)

    def one(block, carry):
        rows = pl.multiple_of(block * per, per)
        wide[pl.ds(rows + per, per)] = gathered[pl.ds(rows, per)].astype(jnp.float32)
        return carry

    lax.fori_loop(0, LOCAL, one, 0)


def stack_tile(tile, wide, table, plus, minus, beams):
    per = 2 * F
    for f0 in range(8):
        f = tile * 8 + f0
        parts = []
        for c in range(2):
            left = wide[pl.ds(c * F + f, PAD_ROWS, stride=per), :]
            right = wide[pl.ds(per + c * F + f, PAD_ROWS, stride=per), :]
            parts.append(jnp.concatenate([left, right], axis=1))
        frames = jnp.concatenate(parts, axis=0).astype(jnp.bfloat16)
        out = jnp.dot(frames, table[f], preferred_element_type=jnp.float32)
        a_re, b_re = out[:PAD_ROWS, :128], out[:PAD_ROWS, 128:]
        a_im, b_im = out[PAD_ROWS:, :128], out[PAD_ROWS:, 128:]
        plus[pl.ds(f0, PAD_ROWS, stride=16), :] = a_re + b_im
        plus[pl.ds(8 + f0, PAD_ROWS, stride=16), :] = a_im - b_re
        minus[pl.ds(f0, PAD_ROWS, stride=16), :] = a_re - b_im
        minus[pl.ds(8 + f0, PAD_ROWS, stride=16), :] = a_im + b_re
    rows = pl.ds(pl.multiple_of(tile * 16, 16), 16)
    beams[:, rows, 0:128] = plus[...].reshape(PAD_ROWS, 16, 128).astype(jnp.bfloat16)
    beams[:, rows, 128:256] = minus[...].reshape(PAD_ROWS, 16, 128).astype(jnp.bfloat16)


def project_one(m, r, first_bin, beams, slowness, tabs, eighth, total):
    def row(ref, *at):
        return jnp.broadcast_to(ref[at + (pl.ds(r, 1), slice(None))], (8, N))

    def packed(value):
        return jnp.concatenate([value, value], axis=0).astype(jnp.bfloat16)

    lower = packed(row(tabs, m, 0) - float(HALF))
    weight = row(tabs, m, 1) * (1.0 / WSTEPS)
    rising, falling = packed(1.0 - weight), packed(1.0 + weight)
    tiles = []
    for q in range(16):
        at = slowness[q * 16:(q + 1) * 16, :]
        gap = jnp.concatenate([at, at], axis=1) - lower
        tiles.append(jnp.maximum(jnp.minimum(gap + rising, falling - gap), jnp.bfloat16(0)))
    hat = jnp.concatenate(tiles, axis=0)
    value = jnp.dot(beams[r], hat, preferred_element_type=jnp.float32)
    bins = (first_bin + lax.broadcasted_iota(jnp.int32, (8, N), 0)).astype(jnp.float32)
    cos0, sin0 = unit_circle(row(tabs, m, 2) * bins, float(NT))
    cos8, sin8 = row(eighth, 0), row(eighth, 1)
    cos1, sin1 = cos0 * cos8 - sin0 * sin8, sin0 * cos8 + cos0 * sin8
    twice = cos8 + cos8
    for t in range(FT):
        re, im = value[t * 16:t * 16 + 8], value[t * 16 + 8:t * 16 + 16]
        total[t * 16:t * 16 + 8, :] += re * cos0 - im * sin0
        total[t * 16 + 8:t * 16 + 16, :] += re * sin0 + im * cos0
        cos0, sin0, cos1, sin1 = cos1, sin1, twice * cos1 - cos0, twice * sin1 - sin0


def kernel(spectra, slow_bins, weight_steps, delays, slowness, node_spectra, power,
           gathered, table, wide, plus, minus, beams, outgoing, tabs, eighth, total, sent, landed, mine, theirs,
           ag_send, ag_recv, tab_send, tab_recv, sum_send, sum_recv, pow_send, pow_recv):
    z, y, x = places()
    freq = lax.axis_index("freq")
    first_bin = BIN0 + freq * F
    barrier = pltpu.get_barrier_semaphore()
    greet = [cable_id(z, y, (x + 1) % X), cable_id(z, y, (x + X - 1) % X),
             cable_id(z, (y + 1) % Y, x), cable_id(z, (y + Y - 1) % Y, x)]
    greet += [cable_id((z + i) % Z, y, x) for i in range(1, Z)]
    greet += [{"freq": (freq + i) % FREQ_DEV} for i in range(1, FREQ_DEV)]
    for device in greet:
        pl.semaphore_signal(barrier, inc=1, device_id=device, device_id_type=MESH)

    own = y * X + x
    for b in range(BLOCKS):
        for c in range(2):
            block = spectra[c, b * STRIDE:(b + 1) * STRIDE, :].astype(jnp.float32)
            rows = pl.multiple_of(own * SHARD + (b * 2 + c) * F, F)
            gathered[pl.ds(rows, F), :] = block.T.astype(jnp.bfloat16)
    for i, source in enumerate((slow_bins, weight_steps, delays)):
        for to in range(Z):
            if to == 0:
                outgoing[0, i, 0:1, :] = jnp.full((1, N), -2000.0 if i == 0 else 0.0, jnp.float32)
                outgoing[0, i, 1:ROWS, :] = source[0:LOCAL, :].astype(jnp.float32)
            else:
                outgoing[to, i, 0:ROWS, :] = source[to * LOCAL - 1:(to + 1) * LOCAL, :].astype(jnp.float32)
            outgoing[to, i, ROWS:PAD_ROWS, :] = jnp.zeros((PAD_ROWS - ROWS, N), jnp.float32)
    pl.semaphore_wait(barrier, len(greet))

    half, quarter = SHARD // 2, SHARD // 4

    def shifted(way, dx, dy):
        if way == 0:
            return (y + Y + dy) % Y, (x + X + dx) % X
        return (y + Y + dx) % Y, (x + X + dy) % X

    def piece(way, owner, kind):
        start = (owner[0] * X + owner[1]) * SHARD + way * half
        size = half
        if kind == 2:
            size = quarter
        elif kind == 3:
            start, size = start + quarter, quarter
        return gathered.at[pl.ds(pl.multiple_of(start, quarter), size), :]

    started = []

    def send(way, stage, kind, owner):
        by = 1 if kind in (0, 2) else -1
        to = shifted(way, by, 0) if stage == 0 else shifted(way, 0, by)
        copy = pltpu.make_async_remote_copy(
            src_ref=piece(way, owner, kind), dst_ref=piece(way, owner, kind),
            send_sem=ag_send.at[way, stage, kind], recv_sem=ag_recv.at[way, stage, kind],
            device_id=cable_id(z, *to), device_id_type=MESH)
        copy.start()
        started.append(copy)

    def arrive(way, stage, kind, owner):
        pltpu.make_async_remote_copy(
            src_ref=piece(way, owner, kind), dst_ref=piece(way, owner, kind),
            send_sem=ag_send.at[way, stage, kind], recv_sem=ag_recv.at[way, stage, kind],
            device_id=cable_id(z, y, (x + 1) % X), device_id_type=MESH).wait_recv()

    first = {0: 0, 1: -1, 2: 1, 3: 2}

    for way in range(2):
        send(way, 0, 0, shifted(way, 0, 0))
        send(way, 0, 1, shifted(way, 0, 0))
    for way in range(2):
        send(way, 1, 0, shifted(way, 0, 0))
        send(way, 1, 1, shifted(way, 0, 0))

    tab_copies = []
    for i in range(1, Z):
        to = (z + i) % Z
        copy = pltpu.make_async_remote_copy(
            src_ref=outgoing.at[to], dst_ref=tabs.at[z],
            send_sem=tab_send.at[i - 1], recv_sem=tab_recv.at[i - 1],
            device_id=cable_id(to, y, x), device_id_type=MESH)
        copy.start()
        tab_copies.append(copy)
    tabs[z] = outgoing[z]

    def steer(part, parts):
        def one(f, carry):
            steering(f, first_bin, table)
            return carry

        lax.fori_loop(part * F // parts, (part + 1) * F // parts, one, 0)

    steer(0, 8)
    for way in range(2):
        for kind, j in ((0, 1), (1, 2)):
            owner = shifted(way, first[j], 0)
            arrive(way, 0, kind, owner)
            send(way, 0, 2 + kind, owner)
            send(way, 1 + j, 0, owner)
            send(way, 1 + j, 1, owner)
    steer(1, 8)
    for way in range(2):
        owner = shifted(way, 2, 0)
        arrive(way, 0, 2, owner)
        arrive(way, 0, 3, owner)
        send(way, 4, 0, owner)
        send(way, 4, 1, owner)
    for j in range(4):
        steer(2 + j, 8)
        for way in range(2):
            for kind, by in ((0, -1), (1, 1)):
                owner = shifted(way, first[j], by)
                arrive(way, 1 + j, kind, owner)
                send(way, 1 + j, 2 + kind, owner)
    steer(6, 8)
    steer(7, 8)
    for j in range(4):
        for way in range(2):
            owner = shifted(way, first[j], 2)
            arrive(way, 1 + j, 2, owner)
            arrive(way, 1 + j, 3, owner)

    widen(gathered, wide)

    def one_tile(tile, carry):
        stack_tile(tile, wide, table, plus, minus, beams)
        return carry

    lax.fori_loop(0, FT, one_tile, 0)

    for i in range(1, Z):
        pltpu.make_async_remote_copy(
            src_ref=outgoing.at[z], dst_ref=tabs.at[(z + Z - i) % Z],
            send_sem=tab_send.at[i - 1], recv_sem=tab_recv.at[i - 1],
            device_id=cable_id((z + i) % Z, y, x), device_id_type=MESH).wait_recv()

    sums = []
    for step in range(Z):
        m = (z + 1 + step) % Z
        cos8, sin8 = unit_circle(tabs[m, 2] * 8.0, float(NT))
        eighth[0] = cos8
        eighth[1] = sin8
        total[...] = jnp.zeros_like(total)

        def one_group(g, carry):
            for j in range(GROUP):
                project_one(m, g * GROUP + j, first_bin, beams, slowness, tabs, eighth, total)
            return carry

        lax.fori_loop(0, ROWS // GROUP, one_group, 0)
        if step < Z - 1:
            sent[step] = total[...]
            copy = pltpu.make_async_remote_copy(
                src_ref=sent.at[step], dst_ref=landed.at[step],
                send_sem=sum_send.at[step], recv_sem=sum_recv.at[step],
                device_id=cable_id(m, y, x), device_id_type=MESH)
            copy.start()
            sums.append(copy)

    for copy in sums:
        copy.wait_recv()
    result = (total[...] + landed[0] + landed[1] + landed[2]) * (Z * LOCAL) ** -0.5
    mine[...] = jnp.broadcast_to(jnp.sum(result * result, axis=0, keepdims=True), (8, N))
    power_copies = []
    for i in range(1, FREQ_DEV):
        copy = pltpu.make_async_remote_copy(
            src_ref=mine, dst_ref=theirs.at[i - 1],
            send_sem=pow_send.at[i - 1], recv_sem=pow_recv.at[i - 1],
            device_id={"freq": (freq + i) % FREQ_DEV}, device_id_type=MESH)
        copy.start()
        power_copies.append(copy)
    split = result.reshape(FT, 2, 8, N)
    for c in range(2):
        part = split[:, c].reshape(F, N)
        node_spectra[:, c, :] = part.T
    for copy in power_copies:
        copy.wait_recv()
    power[...] = (mine[0:1] + theirs[0, 0:1] + theirs[1, 0:1] + theirs[2, 0:1]) * (1.0 / (F * FREQ_DEV))
    for copy in started + tab_copies + sums + power_copies:
        copy.wait_send()


def slowness_rows():
    s = np.full((256, 128), 4000.0, np.float32)
    s[0:HALF + 1] = np.arange(HALF + 1)[:, None]
    s[129:129 + HALF] = -np.arange(1, HALF + 1)[:, None]
    return jnp.asarray(s, jnp.bfloat16)


def shards(spectra, slow_bins, weight_steps, delays):
    vmem = pl.BlockSpec(memory_space=pltpu.VMEM)
    f32, bf16, dma = jnp.float32, jnp.bfloat16, pltpu.SemaphoreType.DMA
    node_spectra, power = pl.pallas_call(
        kernel,
        out_shape=(jax.ShapeDtypeStruct((N, 2, F), f32), jax.ShapeDtypeStruct((1, N), f32)),
        in_specs=[vmem] * 5,
        out_specs=(vmem, vmem),
        scratch_shapes=[
            pltpu.VMEM((PLANE * SHARD, 128), bf16),
            pltpu.VMEM((F, 256, 256), bf16),
            pltpu.VMEM(((PAD_ROWS + 1) * 2 * F, 128), f32),
            pltpu.VMEM((PAD_ROWS * 16, 128), f32),
            pltpu.VMEM((PAD_ROWS * 16, 128), f32),
            pltpu.VMEM((PAD_ROWS, 2 * F, 256), bf16),
            pltpu.VMEM((Z, 3, PAD_ROWS, N), f32),
            pltpu.VMEM((Z, 3, PAD_ROWS, N), f32),
            pltpu.VMEM((2, PAD_ROWS, N), f32),
            pltpu.VMEM((2 * F, N), f32),
            pltpu.VMEM((Z - 1, 2 * F, N), f32),
            pltpu.VMEM((Z - 1, 2 * F, N), f32),
            pltpu.VMEM((8, N), f32),
            pltpu.VMEM((FREQ_DEV - 1, 8, N), f32),
            dma((2, 5, 4)),
            dma((2, 5, 4)),
            dma((Z - 1,)),
            dma((Z - 1,)),
            dma((Z - 1,)),
            dma((Z - 1,)),
            dma((FREQ_DEV - 1,)),
            dma((FREQ_DEV - 1,)),
        ],
        compiler_params=pltpu.CompilerParams(
            collective_id=0, has_side_effects=True, vmem_limit_bytes=60 * 1024 * 1024
        ),
    )(spectra, slow_bins, weight_steps, delays, slowness_rows())
    return node_spectra, power.reshape(N)


def solution(mesh):
    placed = (P(None, "cable", "freq"), P(None, "cable"), P(None, "cable"), P(None, "cable"))
    return jax.shard_map(
        shards,
        mesh=mesh,
        in_specs=placed,
        out_specs=(P("cable", None, "freq"), P("cable")),
        check_vma=False,
    )
```

```python
import functools
import math

import jax
import jax.numpy as jnp
import numpy as np
from jax import lax
from jax.experimental import pallas as pl
from jax.experimental.pallas import tpu as pltpu
from jax.sharding import PartitionSpec as P

SUB_LEN = 256
SLOW = 201
NT = 2000
BIN0 = 20
WSTEPS = 64
HALF = SLOW // 2
STRIDE = SUB_LEN // 2

Z, Y, X = 4, 4, 4
PLANE = Y * X
FREQ_DEV = 4
F = 128
N = 256
BLOCKS = 3
SHARD = BLOCKS * 2 * F
LOCAL = BLOCKS * PLANE
ROWS = LOCAL + 1
PAD_ROWS = 56
FT = F // 8
CHUNKS = 2
CF = F // CHUNKS
CT = CF // 8
CROWS = SHARD // CHUNKS
PER = 2 * CF + 8
STEP = 24
WIDE = 4
TAB_ROWS = 64
GROUP = 7
MESH = pl.DeviceIdType.MESH


def power_series(fun, degree):
    fit = np.polynomial.chebyshev.Chebyshev.interpolate(fun, degree, domain=[0.0, 0.25])
    return [float(c) for c in fit.convert(kind=np.polynomial.Polynomial, domain=[-1, 1], window=[-1, 1]).coef]


COS_TERMS = power_series(lambda v: np.cos(2 * np.pi * np.sqrt(v)), 7)
SIN_TERMS = power_series(lambda v: 2 * np.pi * np.sinc(2 * np.sqrt(v)), 6)


def horner(v, terms):
    total = jnp.full_like(v, terms[-1])
    for term in terms[-2::-1]:
        total = total * v + term
    return total


def unit_circle(count, period):
    rest = count - jnp.round(count * (1.0 / period)) * period
    turns = rest * (1.0 / period)
    v = turns * turns
    return horner(v, COS_TERMS), horner(v, SIN_TERMS) * turns


def places():
    cable = lax.axis_index("cable")
    z = cable // PLANE
    y = (cable // X) % Y
    x = cable % X
    return z, y, x


def cable_id(z, y, x):
    return {"cable": (z * Y + y) * X + x}


def steering(group, first_bin, table):
    period = float(50 * NT)
    k = lax.broadcasted_iota(jnp.int32, (8, 128), 0).astype(jnp.float32)
    s = lax.broadcasted_iota(jnp.int32, (8, 128), 1).astype(jnp.float32)
    factor = SUB_LEN ** -0.5
    state = []
    for u in range(WIDE):
        bs = s * (first_bin + group * WIDE + u).astype(jnp.float32)
        cos0, sin0 = unit_circle(bs * k, period)
        cos8, sin8 = unit_circle(bs * 8.0, period)
        cos0, sin0 = cos0 * factor, sin0 * factor
        state.append((cos0, sin0, cos0 * cos8 - sin0 * sin8, sin0 * cos8 + cos0 * sin8, cos8 + cos8))
    for step in range(SUB_LEN // 16):
        rows = pl.ds(step * 16, 16)
        for u in range(WIDE):
            cos0, sin0, cos1, sin1, twice = state[u]
            table[group * WIDE + u, rows, 0:128] = jnp.concatenate([cos0, cos1], axis=0).astype(jnp.bfloat16)
            table[group * WIDE + u, rows, 128:256] = jnp.concatenate([sin0, sin1], axis=0).astype(jnp.bfloat16)
            cos0, sin0 = twice * cos1 - cos0, twice * sin1 - sin0
            cos1, sin1 = twice * cos0 - cos1, twice * sin0 - sin1
            state[u] = cos0, sin0, cos1, sin1, twice


def widen(chunk, gathered, wide):
    wide[0:2 * CF] = jnp.zeros((2 * CF, 128), jnp.float32)
    wide[(LOCAL + 1) * PER:(LOCAL + 1) * PER + 2 * CF] = jnp.zeros((2 * CF, 128), jnp.float32)

    def one(device, carry):
        for b in range(BLOCKS):
            source = pl.multiple_of(device * SHARD + chunk * CROWS + b * 2 * CF, 2 * CF)
            target = pl.multiple_of((device * BLOCKS + b + 1) * PER, 8)
            wide[pl.ds(target, 2 * CF)] = gathered[pl.ds(source, 2 * CF)].astype(jnp.float32)
        return carry

    lax.fori_loop(0, PLANE, one, 0)


def stack_tile(chunk, tile, wide, table, plus, minus, beams):
    for f0 in range(8):
        at = tile * 8 + f0
        parts = []
        for c in range(2):
            left = wide[pl.ds(c * CF + at, PAD_ROWS, stride=PER), :]
            right = wide[pl.ds(PER + c * CF + at, PAD_ROWS, stride=PER), :]
            parts.append(jnp.concatenate([left, right], axis=1))
        frames = jnp.concatenate(parts, axis=0).astype(jnp.bfloat16)
        out = jnp.dot(frames, table[chunk * CF + at], preferred_element_type=jnp.float32)
        a_re, b_re = out[:PAD_ROWS, :128], out[:PAD_ROWS, 128:]
        a_im, b_im = out[PAD_ROWS:, :128], out[PAD_ROWS:, 128:]
        plus[pl.ds(f0, PAD_ROWS, stride=STEP), :] = a_re + b_im
        plus[pl.ds(8 + f0, PAD_ROWS, stride=STEP), :] = a_im - b_re
        minus[pl.ds(f0, PAD_ROWS, stride=STEP), :] = a_re - b_im
        minus[pl.ds(8 + f0, PAD_ROWS, stride=STEP), :] = a_im + b_re
    rows = pl.ds(pl.multiple_of((chunk * CT + tile) * 16, 16), 16)
    for side, sorted_beams in enumerate((plus, minus)):
        block = sorted_beams[...].reshape(PAD_ROWS, STEP, 128)[:ROWS, :16]
        beams[:, rows, side * 128:(side + 1) * 128] = block.astype(jnp.bfloat16)


def table_row(ref, r, *at):
    return jnp.broadcast_to(ref[at + (pl.ds(r, 1), slice(None))], (8, N))


def hat_of(m, r, slowness, tabs):
    def packed(value):
        return jnp.concatenate([value, value], axis=0).astype(jnp.bfloat16)

    lower = packed(table_row(tabs, r, m, 0) - float(HALF))
    weight = table_row(tabs, r, m, 1) * (1.0 / WSTEPS)
    rising, falling = packed(1.0 - weight), packed(1.0 + weight)
    tiles = []
    for q in range(16):
        at = slowness[q * 16:(q + 1) * 16, :]
        gap = jnp.concatenate([at, at], axis=1) - lower
        tiles.append(jnp.maximum(jnp.minimum(gap + rising, falling - gap), jnp.bfloat16(0)))
    return jnp.concatenate(tiles, axis=0)


def prepare_one(m, r, slot, first_bin, slowness, tabs, hats, starts):
    if slot is not None:
        hats[slot, r] = hat_of(m, r, slowness, tabs)
    bins = (first_bin + lax.broadcasted_iota(jnp.int32, (8, N), 0)).astype(jnp.float32)
    cos0, sin0 = unit_circle(table_row(tabs, r, m, 2) * bins, float(NT))
    starts[m, r, 0:8] = cos0
    starts[m, r, 8:16] = sin0


def project_one(m, r, hat, beams, starts, eighth, total):
    value = jnp.dot(beams[r], hat, preferred_element_type=jnp.float32)
    cos0, sin0 = starts[m, r, 0:8], starts[m, r, 8:16]
    cos8, sin8 = table_row(eighth, r, 0), table_row(eighth, r, 1)
    cos1, sin1 = cos0 * cos8 - sin0 * sin8, sin0 * cos8 + cos0 * sin8
    twice = cos8 + cos8
    for t in range(FT):
        re, im = value[t * 16:t * 16 + 8], value[t * 16 + 8:t * 16 + 16]
        total[t * 16:t * 16 + 8, :] += re * cos0 - im * sin0
        total[t * 16 + 8:t * 16 + 16, :] += re * sin0 + im * cos0
        cos0, sin0, cos1, sin1 = cos1, sin1, twice * cos1 - cos0, twice * sin1 - sin0


def kernel(spectra, slow_bins, weight_steps, delays, slowness, node_spectra, power,
           gathered, table, wide, plus, minus, beams, hats, starts, outgoing, incoming, tabs, eighth, total, sent, landed,
           mine, theirs,
           ag_send, ag_recv, tab_send, tab_recv, sum_send, sum_recv, pow_send, pow_recv):
    z, y, x = places()
    freq = lax.axis_index("freq")
    first_bin = BIN0 + freq * F
    barrier = pltpu.get_barrier_semaphore()
    greet = [cable_id(z, y, (x + 1) % X), cable_id(z, y, (x + X - 1) % X),
             cable_id(z, (y + 1) % Y, x), cable_id(z, (y + Y - 1) % Y, x)]
    greet += [cable_id((z + i) % Z, y, x) for i in range(1, Z)]
    greet += [{"freq": (freq + i) % FREQ_DEV} for i in range(1, FREQ_DEV)]
    for device in greet:
        pl.semaphore_signal(barrier, inc=1, device_id=device, device_id_type=MESH)

    own = y * X + x
    for b in range(BLOCKS):
        for c in range(2):
            block = spectra[c, b * STRIDE:(b + 1) * STRIDE, :].astype(jnp.float32).T.astype(jnp.bfloat16)
            for q in range(CHUNKS):
                rows = pl.multiple_of(own * SHARD + q * CROWS + (b * 2 + c) * CF, CF)
                gathered[pl.ds(rows, CF), :] = block[q * CF:(q + 1) * CF]
    pl.semaphore_wait(barrier, len(greet))

    half, quarter = CROWS // 2, CROWS // 4

    def shifted(way, dx, dy):
        if way == 0:
            return (y + Y + dy) % Y, (x + X + dx) % X
        return (y + Y + dx) % Y, (x + X + dy) % X

    started = []

    def transfer(q, way, stage, kind, owner):
        by = 1 if kind in (0, 2) else -1
        to = shifted(way, by, 0) if stage == 0 else shifted(way, 0, by)
        start = (owner[0] * X + owner[1]) * SHARD + q * CROWS + way * half + (quarter if kind == 3 else 0)
        piece = gathered.at[pl.ds(pl.multiple_of(start, 16), half if kind < 2 else quarter), :]
        return pltpu.make_async_remote_copy(
            src_ref=piece, dst_ref=piece,
            send_sem=ag_send.at[q, way, stage, kind], recv_sem=ag_recv.at[q, way, stage, kind],
            device_id=cable_id(z, *to), device_id_type=MESH)

    def send(q, way, stage, kind, owner):
        copy = transfer(q, way, stage, kind, owner)
        copy.start()
        started.append(copy)

    def arrive(q, way, stage, kind, owner):
        transfer(q, way, stage, kind, owner).wait_recv()

    first = {0: 0, 1: -1, 2: 1, 3: 2}

    def send_own(q):
        for stage in range(2):
            for way in range(2):
                for kind in range(2):
                    send(q, way, stage, kind, shifted(way, 0, 0))

    def from_neighbours(q):
        for way in range(2):
            for kind, j in ((0, 1), (1, 2)):
                owner = shifted(way, first[j], 0)
                arrive(q, way, 0, kind, owner)
                send(q, way, 0, 2 + kind, owner)
                send(q, way, 1 + j, 0, owner)
                send(q, way, 1 + j, 1, owner)

    def from_across(q):
        for way in range(2):
            owner = shifted(way, 2, 0)
            arrive(q, way, 0, 2, owner)
            arrive(q, way, 0, 3, owner)
            send(q, way, 4, 0, owner)
            send(q, way, 4, 1, owner)

    def pass_on(q, j):
        for way in range(2):
            for kind, by in ((0, -1), (1, 1)):
                owner = shifted(way, first[j], by)
                arrive(q, way, 1 + j, kind, owner)
                send(q, way, 1 + j, 2 + kind, owner)

    def last_pieces(q):
        for j in range(4):
            for way in range(2):
                owner = shifted(way, first[j], 2)
                arrive(q, way, 1 + j, 2, owner)
                arrive(q, way, 1 + j, 3, owner)

    def steer(part, parts):
        def one(group, carry):
            steering(group, first_bin, table)
            return carry

        lax.fori_loop(part * (F // WIDE) // parts, (part + 1) * (F // WIDE) // parts, one, 0)

    def tables_from(i):
        source = (z + Z - i) % Z
        if i == 0:
            incoming[z] = outgoing[z]
        else:
            pltpu.make_async_remote_copy(
                src_ref=outgoing.at[z], dst_ref=incoming.at[source],
                send_sem=tab_send.at[i - 1], recv_sem=tab_recv.at[i - 1],
                device_id=cable_id((z + i) % Z, y, x), device_id_type=MESH).wait_recv()
        for k in range(3):
            tabs[source, k] = incoming[source, k].astype(jnp.float32)[:PAD_ROWS]

    def prepare(m, slot):
        def one(g, carry):
            for j in range(GROUP):
                prepare_one(m, g * GROUP + j, slot, first_bin, slowness, tabs, hats, starts)
            return carry

        lax.fori_loop(0, ROWS // GROUP, one, 0)

    def stack(q, begin, end):
        def one_tile(tile, carry):
            stack_tile(q, tile, wide, table, plus, minus, beams)
            return carry

        lax.fori_loop(begin, end, one_tile, 0)

    send_own(0)
    for i, source in enumerate((slow_bins, weight_steps, delays)):
        for to in range(Z):
            if to == 0:
                head = jnp.full((1, N), -2000 if i == 0 else 0, jnp.int32)
                rows = jnp.concatenate([head, source[0:LOCAL, :]], axis=0)
            else:
                rows = source[to * LOCAL - 1:(to + 1) * LOCAL, :]
            rows = jnp.concatenate([rows, jnp.zeros((TAB_ROWS - ROWS, N), jnp.int32)], axis=0)
            outgoing[to, i] = rows.astype(jnp.int16)
    tab_copies = []
    for i in range(1, Z):
        copy = pltpu.make_async_remote_copy(
            src_ref=outgoing.at[(z + i) % Z], dst_ref=incoming.at[z],
            send_sem=tab_send.at[i - 1], recv_sem=tab_recv.at[i - 1],
            device_id=cable_id((z + i) % Z, y, x), device_id_type=MESH)
        copy.start()
        tab_copies.append(copy)
    steer(0, 4)
    from_neighbours(0)
    steer(1, 4)
    send_own(1)
    from_across(0)
    steer(2, 4)
    pass_on(0, 0)
    steer(3, 4)
    pass_on(0, 1)
    pass_on(0, 2)
    tables_from(0)
    prepare(z, 0)
    pass_on(0, 3)
    from_neighbours(1)
    for i in range(1, Z):
        tables_from(i)
    prepare((z + 1) % Z, 1)
    from_across(1)
    prepare((z + 2) % Z, 2)
    last_pieces(0)
    pass_on(1, 0)
    widen(0, gathered, wide)
    stack(0, 0, CT // 2)
    pass_on(1, 1)
    pass_on(1, 2)
    stack(0, CT // 2, CT)
    pass_on(1, 3)
    prepare((z + 3) % Z, None)
    last_pieces(1)
    widen(1, gathered, wide)
    stack(1, 0, CT)

    sums = []
    for step in range(Z):
        m = (z + 1 + step) % Z
        cos8, sin8 = unit_circle(tabs[m, 2] * 8.0, float(NT))
        eighth[0] = cos8
        eighth[1] = sin8
        total[...] = jnp.zeros_like(total)

        def one_group(g, carry):
            for j in range(GROUP):
                r = g * GROUP + j
                hat = hat_of(m, r, slowness, tabs) if step == 2 else hats[(step + 1) % Z, r]
                project_one(m, r, hat, beams, starts, eighth, total)
            return carry

        lax.fori_loop(0, ROWS // GROUP, one_group, 0)
        if step < Z - 1:
            sent[step] = total[...].astype(jnp.bfloat16)
            copy = pltpu.make_async_remote_copy(
                src_ref=sent.at[step], dst_ref=landed.at[step],
                send_sem=sum_send.at[step], recv_sem=sum_recv.at[step],
                device_id=cable_id(m, y, x), device_id_type=MESH)
            copy.start()
            sums.append(copy)

    for copy in sums:
        copy.wait_recv()
    others = (landed[0].astype(jnp.float32) + landed[1].astype(jnp.float32)) + landed[2].astype(jnp.float32)
    result = (total[...] + others) * (Z * LOCAL) ** -0.5
    mine[...] = jnp.broadcast_to(jnp.sum(result * result, axis=0, keepdims=True), (8, N))
    power_copies = []
    for i in range(1, FREQ_DEV):
        copy = pltpu.make_async_remote_copy(
            src_ref=mine, dst_ref=theirs.at[i - 1],
            send_sem=pow_send.at[i - 1], recv_sem=pow_recv.at[i - 1],
            device_id={"freq": (freq + i) % FREQ_DEV}, device_id_type=MESH)
        copy.start()
        power_copies.append(copy)
    split = result.reshape(FT, 2, 8, N)
    for c in range(2):
        part = split[:, c].reshape(F, N)
        node_spectra[:, c, :] = part.T
    for copy in power_copies:
        copy.wait_recv()
    power[...] = (mine[0:1] + theirs[0, 0:1] + theirs[1, 0:1] + theirs[2, 0:1]) * (1.0 / (F * FREQ_DEV))
    for copy in started + tab_copies + sums + power_copies:
        copy.wait_send()


def slowness_rows():
    s = np.full((256, 128), 4000.0, np.float32)
    s[0:HALF + 1] = np.arange(HALF + 1)[:, None]
    s[129:129 + HALF] = -np.arange(1, HALF + 1)[:, None]
    return jnp.asarray(s, jnp.bfloat16)


def shards(spectra, slow_bins, weight_steps, delays):
    vmem = pl.BlockSpec(memory_space=pltpu.VMEM)
    f32, bf16, dma = jnp.float32, jnp.bfloat16, pltpu.SemaphoreType.DMA
    node_spectra, power = pl.pallas_call(
        kernel,
        out_shape=(jax.ShapeDtypeStruct((N, 2, F), f32), jax.ShapeDtypeStruct((1, N), f32)),
        in_specs=[vmem] * 5,
        out_specs=(vmem, vmem),
        scratch_shapes=[
            pltpu.VMEM((PLANE * SHARD, 128), bf16),
            pltpu.VMEM((F, 256, 256), bf16),
            pltpu.VMEM(((PAD_ROWS + 1) * PER, 128), f32),
            pltpu.VMEM((PAD_ROWS * STEP, 128), f32),
            pltpu.VMEM((PAD_ROWS * STEP, 128), f32),
            pltpu.VMEM((ROWS, 2 * F, 256), bf16),
            pltpu.VMEM((Z - 1, ROWS, 256, N), bf16),
            pltpu.VMEM((Z, ROWS, 16, N), f32),
            pltpu.VMEM((Z, 3, TAB_ROWS, N), jnp.int16),
            pltpu.VMEM((Z, 3, TAB_ROWS, N), jnp.int16),
            pltpu.VMEM((Z, 3, PAD_ROWS, N), f32),
            pltpu.VMEM((2, PAD_ROWS, N), f32),
            pltpu.VMEM((2 * F, N), f32),
            pltpu.VMEM((Z - 1, 2 * F, N), bf16),
            pltpu.VMEM((Z - 1, 2 * F, N), bf16),
            pltpu.VMEM((8, N), f32),
            pltpu.VMEM((FREQ_DEV - 1, 8, N), f32),
            dma((CHUNKS, 2, 5, 4)),
            dma((CHUNKS, 2, 5, 4)),
            dma((Z - 1,)),
            dma((Z - 1,)),
            dma((Z - 1,)),
            dma((Z - 1,)),
            dma((FREQ_DEV - 1,)),
            dma((FREQ_DEV - 1,)),
        ],
        compiler_params=pltpu.CompilerParams(
            collective_id=0, has_side_effects=True, vmem_limit_bytes=63 * 1024 * 1024
        ),
    )(spectra, slow_bins, weight_steps, delays, slowness_rows())
    return node_spectra, power.reshape(N)


def solution(mesh):
    placed = (P(None, "cable", "freq"), P(None, "cable"), P(None, "cable"), P(None, "cable"))
    return jax.shard_map(
        shards,
        mesh=mesh,
        in_specs=placed,
        out_specs=(P("cable", None, "freq"), P("cable")),
        check_vma=False,
    )
```

```python
import functools
import math

import jax
import jax.numpy as jnp
import numpy as np
from jax import lax
from jax.experimental import pallas as pl
from jax.experimental.pallas import tpu as pltpu
from jax.sharding import PartitionSpec as P

SUB_LEN = 256
SLOW = 201
NT = 2000
BIN0 = 20
WSTEPS = 64
HALF = SLOW // 2
STRIDE = SUB_LEN // 2

Z, Y, X = 4, 4, 4
PLANE = Y * X
FREQ_DEV = 4
F = 128
N = 256
BLOCKS = 3
SHARD = BLOCKS * 2 * F
LOCAL = BLOCKS * PLANE
ROWS = LOCAL + 1
PAD_ROWS = 56
FT = F // 8
CHUNK_BINS = (96, 32)
CHUNKS = len(CHUNK_BINS)
PER = 2 * max(CHUNK_BINS) + 8
STEP = 24
WIDE = 4
TAB_ROWS = 64
GROUP = 7
MESH = pl.DeviceIdType.MESH


def power_series(fun, degree):
    fit = np.polynomial.chebyshev.Chebyshev.interpolate(fun, degree, domain=[0.0, 0.25])
    return [float(c) for c in fit.convert(kind=np.polynomial.Polynomial, domain=[-1, 1], window=[-1, 1]).coef]


COS_TERMS = power_series(lambda v: np.cos(2 * np.pi * np.sqrt(v)), 7)
SIN_TERMS = power_series(lambda v: 2 * np.pi * np.sinc(2 * np.sqrt(v)), 6)


def horner(v, terms):
    total = jnp.full_like(v, terms[-1])
    for term in terms[-2::-1]:
        total = total * v + term
    return total


def unit_circle(count, period):
    rest = count - jnp.round(count * (1.0 / period)) * period
    turns = rest * (1.0 / period)
    v = turns * turns
    return horner(v, COS_TERMS), horner(v, SIN_TERMS) * turns


def places():
    cable = lax.axis_index("cable")
    z = cable // PLANE
    y = (cable // X) % Y
    x = cable % X
    return z, y, x


def cable_id(z, y, x):
    return {"cable": (z * Y + y) * X + x}


def offset_of(step):
    return 2 - step + 3 * (step // 2) - 2 * (step // 3)


def chunk_rows(q):
    return 2 * BLOCKS * sum(CHUNK_BINS[:q]), 2 * BLOCKS * CHUNK_BINS[q]


def steering(group, first_bin, table):
    period = float(50 * NT)
    k = lax.broadcasted_iota(jnp.int32, (8, 128), 0).astype(jnp.float32)
    s = lax.broadcasted_iota(jnp.int32, (8, 128), 1).astype(jnp.float32)
    factor = SUB_LEN ** -0.5
    state = []
    for u in range(WIDE):
        bs = s * (first_bin + group * WIDE + u).astype(jnp.float32)
        cos0, sin0 = unit_circle(bs * k, period)
        cos8, sin8 = unit_circle(bs * 8.0, period)
        cos0, sin0 = cos0 * factor, sin0 * factor
        state.append((cos0, sin0, cos0 * cos8 - sin0 * sin8, sin0 * cos8 + cos0 * sin8, cos8 + cos8))
    for step in range(STRIDE // 16):
        rows = pl.ds(step * 16, 16)
        for u in range(WIDE):
            cos0, sin0, cos1, sin1, twice = state[u]
            table[group * WIDE + u, rows, 0:128] = jnp.concatenate([cos0, cos1], axis=0).astype(jnp.bfloat16)
            table[group * WIDE + u, rows, 128:256] = jnp.concatenate([sin0, sin1], axis=0).astype(jnp.bfloat16)
            cos0, sin0 = twice * cos1 - cos0, twice * sin1 - sin0
            cos1, sin1 = twice * cos0 - cos1, twice * sin0 - sin1
            state[u] = cos0, sin0, cos1, sin1, twice


def widen(q, gathered, wide):
    base, count = chunk_rows(q)
    size = count // BLOCKS
    wide[0:size] = jnp.zeros((size, 128), jnp.float32)
    wide[(LOCAL + 1) * PER:(LOCAL + 1) * PER + size] = jnp.zeros((size, 128), jnp.float32)

    def one(device, carry):
        for b in range(BLOCKS):
            source = pl.multiple_of(device * SHARD + base + b * size, 64)
            target = pl.multiple_of((device * BLOCKS + b + 1) * PER, 8)
            wide[pl.ds(target, size)] = gathered[pl.ds(source, size)].astype(jnp.float32)
        return carry

    lax.fori_loop(0, PLANE, one, 0)


def stack_tile(q, tile, first_bin, wide, table, plus, minus, beams):
    bins = CHUNK_BINS[q]
    before = sum(CHUNK_BINS[:q])
    for f0 in range(8):
        at = tile * 8 + f0
        parts = [wide[pl.ds(c * bins + at, PAD_ROWS, stride=PER), :] for c in range(2)]
        frames = jnp.concatenate(parts, axis=0).astype(jnp.bfloat16)
        out = jnp.dot(frames, table[before + at], preferred_element_type=jnp.float32)
        a_re, b_re = out[:PAD_ROWS, :128], out[:PAD_ROWS, 128:]
        a_im, b_im = out[PAD_ROWS:, :128], out[PAD_ROWS:, 128:]
        plus[pl.ds(f0, PAD_ROWS, stride=STEP), :] = a_re + b_im
        plus[pl.ds(8 + f0, PAD_ROWS, stride=STEP), :] = a_im - b_re
        minus[pl.ds(f0, PAD_ROWS, stride=STEP), :] = a_re - b_im
        minus[pl.ds(8 + f0, PAD_ROWS, stride=STEP), :] = a_im + b_re
    bin_of = first_bin + before + tile * 8 + lax.broadcasted_iota(jnp.int32, (8, 128), 0)
    s = lax.broadcasted_iota(jnp.int32, (8, 128), 1)
    turn_re, turn_im = unit_circle((bin_of * s * STRIDE).astype(jnp.float32), float(50 * NT))
    rows = pl.ds(pl.multiple_of((before // 8 + tile) * 16, 16), 16)
    for side, stacked in enumerate((plus, minus)):
        im_part = turn_im if side == 0 else -turn_im
        re, im = stacked[0:8, :], stacked[8:16, :]
        for r in range(ROWS):
            at = (r + 1) * STEP
            next_re, next_im = stacked[at:at + 8, :], stacked[at + 8:at + 16, :]
            both = [re + (turn_re * next_re + im_part * next_im), im + (turn_re * next_im - im_part * next_re)]
            beams[r, rows, side * 128:(side + 1) * 128] = jnp.concatenate(both, axis=0).astype(jnp.bfloat16)
            re, im = next_re, next_im


def table_row(ref, r, *at):
    return jnp.broadcast_to(ref[at + (pl.ds(r, 1), slice(None))], (8, N))


def hat_of(m, r, slowness, tabs):
    def packed(value):
        return jnp.concatenate([value, value], axis=0).astype(jnp.bfloat16)

    lower = packed(table_row(tabs, r, m, 0) - float(HALF))
    weight = table_row(tabs, r, m, 1) * (1.0 / WSTEPS)
    rising, falling = packed(1.0 - weight), packed(1.0 + weight)
    tiles = []
    for q in range(16):
        at = slowness[q * 16:(q + 1) * 16, :]
        gap = jnp.concatenate([at, at], axis=1) - lower
        tiles.append(jnp.maximum(jnp.minimum(gap + rising, falling - gap), jnp.bfloat16(0)))
    return jnp.concatenate(tiles, axis=0)


def prepare_one(m, r, slot, first_bin, slowness, tabs, hats, starts):
    hats[slot, r] = hat_of(m, r, slowness, tabs)
    bins = (first_bin + lax.broadcasted_iota(jnp.int32, (8, N), 0)).astype(jnp.float32)
    cos0, sin0 = unit_circle(table_row(tabs, r, m, 2) * bins, float(NT))
    starts[m, r, 0:8] = cos0
    starts[m, r, 8:16] = sin0


def project_one(m, r, hat, beams, starts, eighth, total):
    value = jnp.dot(beams[r], hat, preferred_element_type=jnp.float32)
    cos0, sin0 = starts[m, r, 0:8], starts[m, r, 8:16]
    cos8, sin8 = table_row(eighth, r, 0), table_row(eighth, r, 1)
    cos1, sin1 = cos0 * cos8 - sin0 * sin8, sin0 * cos8 + cos0 * sin8
    twice = cos8 + cos8
    for t in range(FT):
        re, im = value[t * 16:t * 16 + 8], value[t * 16 + 8:t * 16 + 16]
        total[t * 16:t * 16 + 8, :] += re * cos0 - im * sin0
        total[t * 16 + 8:t * 16 + 16, :] += re * sin0 + im * cos0
        cos0, sin0, cos1, sin1 = cos1, sin1, twice * cos1 - cos0, twice * sin1 - sin0


def kernel(spectra, slow_bins, weight_steps, delays, slowness, node_spectra, power,
           gathered, table, wide, plus, minus, beams, hats, starts, outgoing, incoming, tabs, eighth, total, sent, landed,
           mine, theirs, finished,
           ag_send, ag_recv, tab_send, tab_recv, sum_send, sum_recv, pow_send, pow_recv, out_sem):
    z, y, x = places()
    freq = lax.axis_index("freq")
    first_bin = BIN0 + freq * F
    barrier = pltpu.get_barrier_semaphore()
    greet = [cable_id(z, y, (x + 1) % X), cable_id(z, y, (x + X - 1) % X),
             cable_id(z, (y + 1) % Y, x), cable_id(z, (y + Y - 1) % Y, x),
             cable_id(z, y, (x + 2) % X), cable_id(z, (y + 2) % Y, x)]
    greet += [cable_id((z + i) % Z, y, x) for i in range(1, Z)]
    greet += [{"freq": (freq + i) % FREQ_DEV} for i in range(1, FREQ_DEV)]
    for device in greet:
        pl.semaphore_signal(barrier, inc=1, device_id=device, device_id_type=MESH)

    own = y * X + x
    for b in range(BLOCKS):
        for c in range(2):
            block = spectra[c, b * STRIDE:(b + 1) * STRIDE, :].astype(jnp.float32).T.astype(jnp.bfloat16)
            for q, bins in enumerate(CHUNK_BINS):
                before = sum(CHUNK_BINS[:q])
                rows = pl.multiple_of(own * SHARD + chunk_rows(q)[0] + (b * 2 + c) * bins, 32)
                gathered[pl.ds(rows, bins), :] = block[before:before + bins]
    pl.semaphore_wait(barrier, len(greet))

    def shifted(way, dx, dy):
        if way == 0:
            return (y + Y + dy) % Y, (x + X + dx) % X
        return (y + Y + dx) % Y, (x + X + dy) % X

    started = []
    by_kind = (1, -1, 2)

    def transfer(q, way, stage, kind, owner):
        base, count = chunk_rows(q)
        start, size = base + way * (count // 2), count // 2
        if stage == 0:
            to = shifted(way, by_kind[kind], 0)
        elif q == CHUNKS - 1:
            to = shifted(way, 0, by_kind[kind])
        else:
            to = shifted(way, 0, by_kind[kind % 2])
            if kind >= 2:
                size = count // 4
                start += size * (kind - 2)
        piece = gathered.at[pl.ds(pl.multiple_of((owner[0] * X + owner[1]) * SHARD + start, 16), size), :]
        return pltpu.make_async_remote_copy(
            src_ref=piece, dst_ref=piece,
            send_sem=ag_send.at[q, way, stage, kind], recv_sem=ag_recv.at[q, way, stage, kind],
            device_id=cable_id(z, *to), device_id_type=MESH)

    def send(q, way, stage, kind, owner):
        copy = transfer(q, way, stage, kind, owner)
        copy.start()
        started.append(copy)

    def arrive(q, way, stage, kind, owner):
        transfer(q, way, stage, kind, owner).wait_recv()

    first = (0, -1, 1, 2)

    def send_own(q):
        for way in range(2):
            for kind in range(3):
                send(q, way, 0, kind, shifted(way, 0, 0))
        for way in range(2):
            for kind in range(3 if q == CHUNKS - 1 else 2):
                send(q, way, 1, kind, shifted(way, 0, 0))

    def from_first_axis(q, j):
        for way in range(2):
            owner = shifted(way, first[j], 0)
            arrive(q, way, 0, j - 1, owner)
            for kind in range(3 if q == CHUNKS - 1 else 2):
                send(q, way, 1 + j, kind, owner)

    def pass_on(q, j):
        for way in range(2):
            for kind, by in ((0, -1), (1, 1)):
                owner = shifted(way, first[j], by)
                arrive(q, way, 1 + j, kind, owner)
                send(q, way, 1 + j, 2 + kind, owner)

    def last_pieces(q):
        for j in range(4):
            for way in range(2):
                owner = shifted(way, first[j], 2)
                arrive(q, way, 1 + j, 2, owner)
                if q == CHUNKS - 1:
                    arrive(q, way, 1 + j, 0, shifted(way, first[j], -1))
                    arrive(q, way, 1 + j, 1, shifted(way, first[j], 1))
                else:
                    arrive(q, way, 1 + j, 3, owner)

    def steer(part, parts):
        def one(group, carry):
            steering(group, first_bin, table)
            return carry

        lax.fori_loop(part * (F // WIDE) // parts, (part + 1) * (F // WIDE) // parts, one, 0)

    def tables_from(i):
        source = (z + Z - i) % Z
        if i == 0:
            incoming[z] = outgoing[z]
        else:
            pltpu.make_async_remote_copy(
                src_ref=outgoing.at[z], dst_ref=incoming.at[source],
                send_sem=tab_send.at[i - 1], recv_sem=tab_recv.at[i - 1],
                device_id=cable_id((z + i) % Z, y, x), device_id_type=MESH).wait_recv()
        for k in range(3):
            tabs[source, k] = incoming[source, k].astype(jnp.float32)[:PAD_ROWS]

    def prepare(m, slot):
        def one(g, carry):
            for j in range(GROUP):
                prepare_one(m, g * GROUP + j, slot, first_bin, slowness, tabs, hats, starts)
            return carry

        lax.fori_loop(0, ROWS // GROUP, one, 0)

    def stack(q, begin, end):
        def four_tiles(group, carry):
            for u in range(4):
                stack_tile(q, group * 4 + u, first_bin, wide, table, plus, minus, beams)
            return carry

        lax.fori_loop(begin // 4, end // 4, four_tiles, 0)

    send_own(0)
    for i, source in enumerate((slow_bins, weight_steps, delays)):
        for to in range(Z):
            if to == 0:
                head = jnp.full((1, N), -2000 if i == 0 else 0, jnp.int32)
                rows = jnp.concatenate([head, source[0:LOCAL, :]], axis=0)
            else:
                rows = source[to * LOCAL - 1:(to + 1) * LOCAL, :]
            rows = jnp.concatenate([rows, jnp.zeros((TAB_ROWS - ROWS, N), jnp.int32)], axis=0)
            outgoing[to, i] = rows.astype(jnp.int16)
    tab_copies = []
    for i in range(1, Z):
        copy = pltpu.make_async_remote_copy(
            src_ref=outgoing.at[(z + i) % Z], dst_ref=incoming.at[z],
            send_sem=tab_send.at[i - 1], recv_sem=tab_recv.at[i - 1],
            device_id=cable_id((z + i) % Z, y, x), device_id_type=MESH)
        copy.start()
        tab_copies.append(copy)
    steer(0, 4)
    steer(1, 4)
    from_first_axis(0, 1)
    from_first_axis(0, 2)
    steer(2, 4)
    from_first_axis(0, 3)
    pass_on(0, 0)
    send_own(1)
    steer(3, 4)
    tables_from(0)
    pass_on(0, 1)
    prepare(z, 3)
    pass_on(0, 2)
    from_first_axis(1, 1)
    from_first_axis(1, 2)
    from_first_axis(1, 3)
    pass_on(0, 3)
    for step in range(Z - 1):
        tables_from(Z - offset_of(step))
        prepare((z + offset_of(step)) % Z, step)
    last_pieces(0)
    widen(0, gathered, wide)
    stack(0, 0, CHUNK_BINS[0] // 8)
    last_pieces(1)
    widen(1, gathered, wide)
    stack(1, 0, CHUNK_BINS[1] // 8)

    def sum_copy(step, m):
        return pltpu.make_async_remote_copy(
            src_ref=sent.at[step], dst_ref=landed.at[step],
            send_sem=sum_send.at[step], recv_sem=sum_recv.at[step],
            device_id=cable_id(m, y, x), device_id_type=MESH)

    def one_step(step, carry):
        m = (z + offset_of(step)) % Z
        cos8, sin8 = unit_circle(tabs[m, 2] * 8.0, float(NT))
        eighth[0] = cos8
        eighth[1] = sin8
        total[...] = jnp.zeros_like(total)
        for r in range(ROWS):
            project_one(m, r, hats[step, r], beams, starts, eighth, total)

        @pl.when(step < Z - 1)
        def _():
            sent[step] = total[...].astype(jnp.bfloat16)
            sum_copy(step, m).start()

        return carry

    lax.fori_loop(0, Z, one_step, 0)
    sums = [sum_copy(step, (z + offset_of(step)) % Z) for step in range(Z - 1)]
    for copy in sums:
        copy.wait_recv()
    others = (landed[0].astype(jnp.float32) + landed[1].astype(jnp.float32)) + landed[2].astype(jnp.float32)
    result = (total[...] + others) * (Z * LOCAL) ** -0.5
    mine[...] = jnp.broadcast_to(jnp.sum(result * result, axis=0, keepdims=True), (8, N))
    power_copies = []
    for i in range(1, FREQ_DEV):
        copy = pltpu.make_async_remote_copy(
            src_ref=mine, dst_ref=theirs.at[i - 1],
            send_sem=pow_send.at[i - 1], recv_sem=pow_recv.at[i - 1],
            device_id={"freq": (freq + i) % FREQ_DEV}, device_id_type=MESH)
        copy.start()
        power_copies.append(copy)
    split = result.reshape(FT, 2, 8, N)
    for c in range(2):
        part = split[:, c].reshape(F, N)
        finished[:, c, :] = part.T
    writing = pltpu.make_async_copy(finished, node_spectra, out_sem)
    writing.start()
    for copy in power_copies:
        copy.wait_recv()
    power[...] = (mine[0:1] + theirs[0, 0:1] + theirs[1, 0:1] + theirs[2, 0:1]) * (1.0 / (F * FREQ_DEV))
    for copy in started + tab_copies + sums + power_copies:
        copy.wait_send()
    writing.wait()


def slowness_rows():
    s = np.full((256, 128), 4000.0, np.float32)
    s[0:HALF + 1] = np.arange(HALF + 1)[:, None]
    s[129:129 + HALF] = -np.arange(1, HALF + 1)[:, None]
    return jnp.asarray(s, jnp.bfloat16)


def shards(spectra, slow_bins, weight_steps, delays):
    vmem = pl.BlockSpec(memory_space=pltpu.VMEM)
    f32, bf16, dma = jnp.float32, jnp.bfloat16, pltpu.SemaphoreType.DMA
    node_spectra, power = pl.pallas_call(
        kernel,
        out_shape=(jax.ShapeDtypeStruct((N, 2, F), f32), jax.ShapeDtypeStruct((1, N), f32)),
        in_specs=[vmem] * 5,
        out_specs=(pl.BlockSpec(memory_space=pl.ANY), vmem),
        scratch_shapes=[
            pltpu.VMEM((PLANE * SHARD, 128), bf16),
            pltpu.VMEM((F, STRIDE, 256), bf16),
            pltpu.VMEM((PAD_ROWS * PER, 128), f32),
            pltpu.VMEM((PAD_ROWS * STEP, 128), f32),
            pltpu.VMEM((PAD_ROWS * STEP, 128), f32),
            pltpu.VMEM((ROWS, 2 * F, 256), bf16),
            pltpu.VMEM((Z, ROWS, 256, N), bf16),
            pltpu.VMEM((Z, ROWS, 16, N), f32),
            pltpu.VMEM((Z, 3, TAB_ROWS, N), jnp.int16),
            pltpu.VMEM((Z, 3, TAB_ROWS, N), jnp.int16),
            pltpu.VMEM((Z, 3, PAD_ROWS, N), f32),
            pltpu.VMEM((2, PAD_ROWS, N), f32),
            pltpu.VMEM((2 * F, N), f32),
            pltpu.VMEM((Z - 1, 2 * F, N), bf16),
            pltpu.VMEM((Z - 1, 2 * F, N), bf16),
            pltpu.VMEM((8, N), f32),
            pltpu.VMEM((FREQ_DEV - 1, 8, N), f32),
            pltpu.VMEM((N, 2, F), f32),
            dma((CHUNKS, 2, 5, 4)),
            dma((CHUNKS, 2, 5, 4)),
            dma((Z - 1,)),
            dma((Z - 1,)),
            dma((Z - 1,)),
            dma((Z - 1,)),
            dma((FREQ_DEV - 1,)),
            dma((FREQ_DEV - 1,)),
            dma,
        ],
        compiler_params=pltpu.CompilerParams(
            collective_id=0, has_side_effects=True, vmem_limit_bytes=63 * 1024 * 1024
        ),
    )(spectra, slow_bins, weight_steps, delays, slowness_rows())
    return node_spectra, power.reshape(N)


def solution(mesh):
    placed = (P(None, "cable", "freq"), P(None, "cable"), P(None, "cable"), P(None, "cable"))
    return jax.shard_map(
        shards,
        mesh=mesh,
        in_specs=placed,
        out_specs=(P("cable", None, "freq"), P("cable")),
        check_vma=False,
    )
```

```python
import functools
import math

import jax
import jax.numpy as jnp
import numpy as np
from jax import lax
from jax.experimental import pallas as pl
from jax.experimental.pallas import tpu as pltpu
from jax.sharding import PartitionSpec as P

SUB_LEN = 256
SLOW = 201
NT = 2000
BIN0 = 20
WSTEPS = 64
HALF = SLOW // 2
STRIDE = SUB_LEN // 2

Z, Y, X = 4, 4, 4
PLANE = Y * X
FREQ_DEV = 4
F = 128
N = 256
BLOCKS = 3
SHARD = BLOCKS * 2 * F
LOCAL = BLOCKS * PLANE
ROWS = LOCAL + 1
PAD_ROWS = 56
FT = F // 8
CHUNK_BINS = (96, 32)
CHUNKS = len(CHUNK_BINS)
PER = 2 * max(CHUNK_BINS) + 8
STEP = 24
WIDE = 4
TAB_ROWS = 64
GROUP = 7
MESH = pl.DeviceIdType.MESH


def power_series(fun, degree):
    fit = np.polynomial.chebyshev.Chebyshev.interpolate(fun, degree, domain=[0.0, 0.25])
    return [float(c) for c in fit.convert(kind=np.polynomial.Polynomial, domain=[-1, 1], window=[-1, 1]).coef]


COS_TERMS = power_series(lambda v: np.cos(2 * np.pi * np.sqrt(v)), 7)
SIN_TERMS = power_series(lambda v: 2 * np.pi * np.sinc(2 * np.sqrt(v)), 6)


def horner(v, terms):
    total = jnp.full_like(v, terms[-1])
    for term in terms[-2::-1]:
        total = total * v + term
    return total


def unit_circle(count, period):
    rest = count - jnp.round(count * (1.0 / period)) * period
    turns = rest * (1.0 / period)
    v = turns * turns
    return horner(v, COS_TERMS), horner(v, SIN_TERMS) * turns


def places():
    cable = lax.axis_index("cable")
    z = cable // PLANE
    y = (cable // X) % Y
    x = cable % X
    return z, y, x


def cable_id(z, y, x):
    return {"cable": (z * Y + y) * X + x}


def offset_of(step):
    return 2 - step + 3 * (step // 2) - 2 * (step // 3)


def chunk_rows(q):
    return 2 * BLOCKS * sum(CHUNK_BINS[:q]), 2 * BLOCKS * CHUNK_BINS[q]


def steering(group, first_bin, table):
    period = float(50 * NT)
    k = lax.broadcasted_iota(jnp.int32, (8, 128), 0).astype(jnp.float32)
    s = lax.broadcasted_iota(jnp.int32, (8, 128), 1).astype(jnp.float32)
    factor = SUB_LEN ** -0.5
    state = []
    for u in range(WIDE):
        bs = s * (first_bin + group * WIDE + u).astype(jnp.float32)
        cos0, sin0 = unit_circle(bs * k, period)
        cos8, sin8 = unit_circle(bs * 8.0, period)
        cos0, sin0 = cos0 * factor, sin0 * factor
        state.append((cos0, sin0, cos0 * cos8 - sin0 * sin8, sin0 * cos8 + cos0 * sin8, cos8 + cos8))
    for step in range(STRIDE // 16):
        rows = pl.ds(step * 16, 16)
        for u in range(WIDE):
            cos0, sin0, cos1, sin1, twice = state[u]
            table[group * WIDE + u, rows, 0:128] = jnp.concatenate([cos0, cos1], axis=0).astype(jnp.bfloat16)
            table[group * WIDE + u, rows, 128:256] = jnp.concatenate([sin0, sin1], axis=0).astype(jnp.bfloat16)
            cos0, sin0 = twice * cos1 - cos0, twice * sin1 - sin0
            cos1, sin1 = twice * cos0 - cos1, twice * sin0 - sin1
            state[u] = cos0, sin0, cos1, sin1, twice


def widen(q, gathered, wide):
    base, count = chunk_rows(q)
    size = count // BLOCKS
    wide[0:size] = jnp.zeros((size, 128), jnp.float32)
    wide[(LOCAL + 1) * PER:(LOCAL + 1) * PER + size] = jnp.zeros((size, 128), jnp.float32)

    def one(device, carry):
        for b in range(BLOCKS):
            source = pl.multiple_of(device * SHARD + base + b * size, 64)
            target = pl.multiple_of((device * BLOCKS + b + 1) * PER, 8)
            wide[pl.ds(target, size)] = gathered[pl.ds(source, size)].astype(jnp.float32)
        return carry

    lax.fori_loop(0, PLANE, one, 0)


def stack_tile(q, tile, first_bin, wide, table, plus, minus, beams):
    bins = CHUNK_BINS[q]
    before = sum(CHUNK_BINS[:q])
    for f0 in range(8):
        at = tile * 8 + f0
        parts = [wide[pl.ds(c * bins + at, PAD_ROWS, stride=PER), :] for c in range(2)]
        frames = jnp.concatenate(parts, axis=0).astype(jnp.bfloat16)
        out = jnp.dot(frames, table[before + at], preferred_element_type=jnp.float32)
        a_re, b_re = out[:PAD_ROWS, :128], out[:PAD_ROWS, 128:]
        a_im, b_im = out[PAD_ROWS:, :128], out[PAD_ROWS:, 128:]
        plus[pl.ds(f0, PAD_ROWS, stride=STEP), :] = a_re + b_im
        plus[pl.ds(8 + f0, PAD_ROWS, stride=STEP), :] = a_im - b_re
        minus[pl.ds(f0, PAD_ROWS, stride=STEP), :] = a_re - b_im
        minus[pl.ds(8 + f0, PAD_ROWS, stride=STEP), :] = a_im + b_re
    bin_of = first_bin + before + tile * 8 + lax.broadcasted_iota(jnp.int32, (8, 128), 0)
    s = lax.broadcasted_iota(jnp.int32, (8, 128), 1)
    turn_re, turn_im = unit_circle((bin_of * s * STRIDE).astype(jnp.float32), float(50 * NT))
    rows = pl.ds(pl.multiple_of((before // 8 + tile) * 16, 16), 16)
    for side, stacked in enumerate((plus, minus)):
        im_part = turn_im if side == 0 else -turn_im
        re, im = stacked[0:8, :], stacked[8:16, :]
        for r in range(ROWS):
            at = (r + 1) * STEP
            next_re, next_im = stacked[at:at + 8, :], stacked[at + 8:at + 16, :]
            both = [re + (turn_re * next_re + im_part * next_im), im + (turn_re * next_im - im_part * next_re)]
            beams[r, rows, side * 128:(side + 1) * 128] = jnp.concatenate(both, axis=0).astype(jnp.bfloat16)
            re, im = next_re, next_im


def table_row(ref, r, *at):
    return jnp.broadcast_to(ref[at + (pl.ds(r, 1), slice(None))], (8, N))


def hat_of(m, r, slowness, tabs):
    def packed(value):
        return jnp.concatenate([value, value], axis=0).astype(jnp.bfloat16)

    bin_row, weight = table_row(tabs, r, m, 0), table_row(tabs, r, m, 1) * (1.0 / WSTEPS)
    lower, upper = packed(bin_row - float(HALF)), packed(bin_row - float(HALF - 1))
    low_part, high_part, none = packed(1.0 - weight), packed(weight), jnp.zeros((16, N), jnp.bfloat16)
    tiles = []
    for q in range(16):
        at = slowness[q * 16:(q + 1) * 16, :]
        at = jnp.concatenate([at, at], axis=1)
        tiles.append(jnp.where(at == lower, low_part, jnp.where(at == upper, high_part, none)))
    return jnp.concatenate(tiles, axis=0)


def prepare_one(m, r, slot, first_bin, slowness, tabs, hats, starts):
    hats[slot, r] = hat_of(m, r, slowness, tabs)
    bins = (first_bin + lax.broadcasted_iota(jnp.int32, (8, N), 0)).astype(jnp.float32)
    cos0, sin0 = unit_circle(table_row(tabs, r, m, 2) * bins, float(NT))
    starts[m, r, 0:8] = cos0
    starts[m, r, 8:16] = sin0


def project_one(m, r, hat, beams, starts, eighth, total):
    value = jnp.dot(beams[r], hat, preferred_element_type=jnp.float32)
    cos0, sin0 = starts[m, r, 0:8], starts[m, r, 8:16]
    cos8, sin8 = table_row(eighth, r, 0), table_row(eighth, r, 1)
    cos1, sin1 = cos0 * cos8 - sin0 * sin8, sin0 * cos8 + cos0 * sin8
    twice = cos8 + cos8
    for t in range(FT):
        re, im = value[t * 16:t * 16 + 8], value[t * 16 + 8:t * 16 + 16]
        total[t * 16:t * 16 + 8, :] += re * cos0 - im * sin0
        total[t * 16 + 8:t * 16 + 16, :] += re * sin0 + im * cos0
        cos0, sin0, cos1, sin1 = cos1, sin1, twice * cos1 - cos0, twice * sin1 - sin0


def kernel(spectra, slow_bins, weight_steps, delays, slowness, node_spectra, power,
           gathered, table, wide, plus, minus, beams, hats, starts, outgoing, incoming, tabs, eighth, total, sent, landed,
           mine, theirs, finished,
           ag_send, ag_recv, tab_send, tab_recv, sum_send, sum_recv, pow_send, pow_recv, out_sem):
    z, y, x = places()
    freq = lax.axis_index("freq")
    first_bin = BIN0 + freq * F
    barrier = pltpu.get_barrier_semaphore()
    greet = [cable_id(z, y, (x + 1) % X), cable_id(z, y, (x + X - 1) % X),
             cable_id(z, (y + 1) % Y, x), cable_id(z, (y + Y - 1) % Y, x),
             cable_id(z, y, (x + 2) % X), cable_id(z, (y + 2) % Y, x)]
    greet += [cable_id((z + i) % Z, y, x) for i in range(1, Z)]
    greet += [{"freq": (freq + i) % FREQ_DEV} for i in range(1, FREQ_DEV)]
    for device in greet:
        pl.semaphore_signal(barrier, inc=1, device_id=device, device_id_type=MESH)

    own = y * X + x
    for b in range(BLOCKS):
        for c in range(2):
            block = spectra[c, b * STRIDE:(b + 1) * STRIDE, :].astype(jnp.float32).T.astype(jnp.bfloat16)
            for q, bins in enumerate(CHUNK_BINS):
                before = sum(CHUNK_BINS[:q])
                rows = pl.multiple_of(own * SHARD + chunk_rows(q)[0] + (b * 2 + c) * bins, 32)
                gathered[pl.ds(rows, bins), :] = block[before:before + bins]
    pl.semaphore_wait(barrier, len(greet))

    def shifted(way, dx, dy):
        if way == 0:
            return (y + Y + dy) % Y, (x + X + dx) % X
        return (y + Y + dx) % Y, (x + X + dy) % X

    started = []
    by_kind = (1, -1, 2)

    def transfer(q, way, stage, kind, owner):
        base, count = chunk_rows(q)
        start, size = base + way * (count // 2), count // 2
        if stage == 0:
            to = shifted(way, by_kind[kind], 0)
        elif q == CHUNKS - 1:
            to = shifted(way, 0, by_kind[kind])
        else:
            to = shifted(way, 0, by_kind[kind % 2])
            if kind >= 2:
                size = count // 4
                start += size * (kind - 2)
        piece = gathered.at[pl.ds(pl.multiple_of((owner[0] * X + owner[1]) * SHARD + start, 16), size), :]
        return pltpu.make_async_remote_copy(
            src_ref=piece, dst_ref=piece,
            send_sem=ag_send.at[q, way, stage, kind], recv_sem=ag_recv.at[q, way, stage, kind],
            device_id=cable_id(z, *to), device_id_type=MESH)

    def send(q, way, stage, kind, owner):
        copy = transfer(q, way, stage, kind, owner)
        copy.start()
        started.append(copy)

    def arrive(q, way, stage, kind, owner):
        transfer(q, way, stage, kind, owner).wait_recv()

    first = (0, -1, 1, 2)

    def send_own(q):
        for way in range(2):
            for kind in range(3):
                send(q, way, 0, kind, shifted(way, 0, 0))
        for way in range(2):
            for kind in range(3 if q == CHUNKS - 1 else 2):
                send(q, way, 1, kind, shifted(way, 0, 0))

    def from_first_axis(q, j):
        for way in range(2):
            owner = shifted(way, first[j], 0)
            arrive(q, way, 0, j - 1, owner)
            for kind in range(3 if q == CHUNKS - 1 else 2):
                send(q, way, 1 + j, kind, owner)

    def pass_on(q, j):
        for way in range(2):
            for kind, by in ((0, -1), (1, 1)):
                owner = shifted(way, first[j], by)
                arrive(q, way, 1 + j, kind, owner)
                send(q, way, 1 + j, 2 + kind, owner)

    def last_pieces(q):
        for j in range(4):
            for way in range(2):
                owner = shifted(way, first[j], 2)
                arrive(q, way, 1 + j, 2, owner)
                if q == CHUNKS - 1:
                    arrive(q, way, 1 + j, 0, shifted(way, first[j], -1))
                    arrive(q, way, 1 + j, 1, shifted(way, first[j], 1))
                else:
                    arrive(q, way, 1 + j, 3, owner)

    def steer(part, parts):
        def one(group, carry):
            steering(group, first_bin, table)
            return carry

        lax.fori_loop(part * (F // WIDE) // parts, (part + 1) * (F // WIDE) // parts, one, 0)

    def tables_from(i):
        source = (z + Z - i) % Z
        if i == 0:
            incoming[z] = outgoing[z]
        else:
            pltpu.make_async_remote_copy(
                src_ref=outgoing.at[z], dst_ref=incoming.at[source],
                send_sem=tab_send.at[i - 1], recv_sem=tab_recv.at[i - 1],
                device_id=cable_id((z + i) % Z, y, x), device_id_type=MESH).wait_recv()
        for k in range(3):
            tabs[source, k] = incoming[source, k].astype(jnp.float32)[:PAD_ROWS]

    def prepare(m, slot):
        def one(g, carry):
            for j in range(GROUP):
                prepare_one(m, g * GROUP + j, slot, first_bin, slowness, tabs, hats, starts)
            return carry

        lax.fori_loop(0, ROWS // GROUP, one, 0)

    def stack(q, begin, end):
        def four_tiles(group, carry):
            for u in range(4):
                stack_tile(q, group * 4 + u, first_bin, wide, table, plus, minus, beams)
            return carry

        lax.fori_loop(begin // 4, end // 4, four_tiles, 0)

    send_own(0)
    for i, source in enumerate((slow_bins, weight_steps, delays)):
        for to in range(Z):
            if to == 0:
                head = jnp.full((1, N), -2000 if i == 0 else 0, jnp.int32)
                rows = jnp.concatenate([head, source[0:LOCAL, :]], axis=0)
            else:
                rows = source[to * LOCAL - 1:(to + 1) * LOCAL, :]
            rows = jnp.concatenate([rows, jnp.zeros((TAB_ROWS - ROWS, N), jnp.int32)], axis=0)
            outgoing[to, i] = rows.astype(jnp.int16)
    tab_copies = []
    for i in (1, 3, 2):
        copy = pltpu.make_async_remote_copy(
            src_ref=outgoing.at[(z + i) % Z], dst_ref=incoming.at[z],
            send_sem=tab_send.at[i - 1], recv_sem=tab_recv.at[i - 1],
            device_id=cable_id((z + i) % Z, y, x), device_id_type=MESH)
        copy.start()
        tab_copies.append(copy)
    steer(0, 4)
    steer(1, 4)
    from_first_axis(0, 1)
    from_first_axis(0, 2)
    steer(2, 4)
    from_first_axis(0, 3)
    pass_on(0, 0)
    send_own(1)
    steer(3, 4)
    tables_from(0)
    pass_on(0, 1)
    prepare(z, 3)
    pass_on(0, 2)
    pass_on(0, 3)
    from_first_axis(1, 1)
    from_first_axis(1, 2)
    from_first_axis(1, 3)
    for step in (2, 1, 0):
        tables_from(Z - offset_of(step))
        prepare((z + offset_of(step)) % Z, step)
    last_pieces(0)
    widen(0, gathered, wide)
    stack(0, 0, CHUNK_BINS[0] // 8)
    last_pieces(1)
    widen(1, gathered, wide)
    stack(1, 0, CHUNK_BINS[1] // 8)

    def sum_copy(step, m):
        return pltpu.make_async_remote_copy(
            src_ref=sent.at[step], dst_ref=landed.at[step],
            send_sem=sum_send.at[step], recv_sem=sum_recv.at[step],
            device_id=cable_id(m, y, x), device_id_type=MESH)

    def one_step(step, carry):
        m = (z + offset_of(step)) % Z
        cos8, sin8 = unit_circle(tabs[m, 2] * 8.0, float(NT))
        eighth[0] = cos8
        eighth[1] = sin8
        total[...] = jnp.zeros_like(total)
        for r in range(ROWS):
            project_one(m, r, hats[step, r], beams, starts, eighth, total)

        @pl.when(step < Z - 1)
        def _():
            sent[step] = total[...].astype(jnp.bfloat16)
            sum_copy(step, m).start()

        return carry

    lax.fori_loop(0, Z, one_step, 0)
    sums = [sum_copy(step, (z + offset_of(step)) % Z) for step in range(Z - 1)]
    for copy in sums:
        copy.wait_recv()
    others = (landed[0].astype(jnp.float32) + landed[1].astype(jnp.float32)) + landed[2].astype(jnp.float32)
    result = (total[...] + others) * (Z * LOCAL) ** -0.5
    mine[...] = jnp.broadcast_to(jnp.sum(result * result, axis=0, keepdims=True), (8, N))
    power_copies = []
    for i in range(1, FREQ_DEV):
        copy = pltpu.make_async_remote_copy(
            src_ref=mine, dst_ref=theirs.at[i - 1],
            send_sem=pow_send.at[i - 1], recv_sem=pow_recv.at[i - 1],
            device_id={"freq": (freq + i) % FREQ_DEV}, device_id_type=MESH)
        copy.start()
        power_copies.append(copy)
    finished[...] = result
    writing = pltpu.make_async_copy(finished, node_spectra, out_sem)
    writing.start()
    for copy in power_copies:
        copy.wait_recv()
    power[...] = (mine[0:1] + theirs[0, 0:1] + theirs[1, 0:1] + theirs[2, 0:1]) * (1.0 / (F * FREQ_DEV))
    for copy in started + tab_copies + sums + power_copies:
        copy.wait_send()
    writing.wait()


def turn_kernel(sums, power_row, node_spectra, power):
    split = sums[...].reshape(FT, 2, 8, N)
    for c in range(2):
        node_spectra[:, c, :] = split[:, c].reshape(F, N).T
    power[...] = power_row[...]


def slowness_rows():
    s = np.full((256, 128), 4000.0, np.float32)
    s[0:HALF + 1] = np.arange(HALF + 1)[:, None]
    s[129:129 + HALF] = -np.arange(1, HALF + 1)[:, None]
    return jnp.asarray(s, jnp.bfloat16)


def shards(spectra, slow_bins, weight_steps, delays):
    vmem = pl.BlockSpec(memory_space=pltpu.VMEM)
    f32, bf16, dma = jnp.float32, jnp.bfloat16, pltpu.SemaphoreType.DMA
    sums, power_row = pl.pallas_call(
        kernel,
        out_shape=(jax.ShapeDtypeStruct((2 * F, N), f32), jax.ShapeDtypeStruct((1, N), f32)),
        in_specs=[vmem] * 5,
        out_specs=(pl.BlockSpec(memory_space=pl.ANY), vmem),
        scratch_shapes=[
            pltpu.VMEM((PLANE * SHARD, 128), bf16),
            pltpu.VMEM((F, STRIDE, 256), bf16),
            pltpu.VMEM((PAD_ROWS * PER, 128), f32),
            pltpu.VMEM((PAD_ROWS * STEP, 128), f32),
            pltpu.VMEM((PAD_ROWS * STEP, 128), f32),
            pltpu.VMEM((ROWS, 2 * F, 256), bf16),
            pltpu.VMEM((Z, ROWS, 256, N), bf16),
            pltpu.VMEM((Z, ROWS, 16, N), f32),
            pltpu.VMEM((Z, 3, TAB_ROWS, N), jnp.int16),
            pltpu.VMEM((Z, 3, TAB_ROWS, N), jnp.int16),
            pltpu.VMEM((Z, 3, PAD_ROWS, N), f32),
            pltpu.VMEM((2, PAD_ROWS, N), f32),
            pltpu.VMEM((2 * F, N), f32),
            pltpu.VMEM((Z - 1, 2 * F, N), bf16),
            pltpu.VMEM((Z - 1, 2 * F, N), bf16),
            pltpu.VMEM((8, N), f32),
            pltpu.VMEM((FREQ_DEV - 1, 8, N), f32),
            pltpu.VMEM((2 * F, N), f32),
            dma((CHUNKS, 2, 5, 4)),
            dma((CHUNKS, 2, 5, 4)),
            dma((Z - 1,)),
            dma((Z - 1,)),
            dma((Z - 1,)),
            dma((Z - 1,)),
            dma((FREQ_DEV - 1,)),
            dma((FREQ_DEV - 1,)),
            dma,
        ],
        compiler_params=pltpu.CompilerParams(
            collective_id=0, has_side_effects=True, vmem_limit_bytes=63 * 1024 * 1024
        ),
    )(spectra, slow_bins, weight_steps, delays, slowness_rows())
    node_spectra, power = pl.pallas_call(
        turn_kernel,
        out_shape=(jax.ShapeDtypeStruct((N, 2, F), f32), jax.ShapeDtypeStruct((1, N), f32)),
        in_specs=[vmem] * 2,
        out_specs=(vmem, vmem),
    )(sums, power_row)
    return node_spectra, power.reshape(N)


def solution(mesh):
    placed = (P(None, "cable", "freq"), P(None, "cable"), P(None, "cable"), P(None, "cable"))
    return jax.shard_map(
        shards,
        mesh=mesh,
        in_specs=placed,
        out_specs=(P("cable", None, "freq"), P("cable")),
        check_vma=False,
    )
```

```python
import functools
import math

import jax
import jax.numpy as jnp
import numpy as np
from jax import lax
from jax.experimental import pallas as pl
from jax.experimental.pallas import tpu as pltpu
from jax.sharding import PartitionSpec as P

SUB_LEN = 256
SLOW = 201
NT = 2000
BIN0 = 20
WSTEPS = 64
HALF = SLOW // 2
STRIDE = SUB_LEN // 2

Z, Y, X = 4, 4, 4
PLANE = Y * X
FREQ_DEV = 4
F = 128
N = 256
BLOCKS = 3
SHARD = BLOCKS * 2 * F
LOCAL = BLOCKS * PLANE
ROWS = LOCAL + 1
PAD_ROWS = 56
FT = F // 8
CHUNK_BINS = (96, 32)
CHUNKS = len(CHUNK_BINS)
PER = 2 * max(CHUNK_BINS) + 8
STEP = 24
WIDE = 4
TAB_ROWS = 64
GROUP = 7
MESH = pl.DeviceIdType.MESH


def power_series(fun, degree):
    fit = np.polynomial.chebyshev.Chebyshev.interpolate(fun, degree, domain=[0.0, 0.25])
    return [float(c) for c in fit.convert(kind=np.polynomial.Polynomial, domain=[-1, 1], window=[-1, 1]).coef]


COS_TERMS = power_series(lambda v: np.cos(2 * np.pi * np.sqrt(v)), 7)
SIN_TERMS = power_series(lambda v: 2 * np.pi * np.sinc(2 * np.sqrt(v)), 6)


def horner(v, terms):
    total = jnp.full_like(v, terms[-1])
    for term in terms[-2::-1]:
        total = total * v + term
    return total


def unit_circle(count, period):
    rest = count - jnp.round(count * (1.0 / period)) * period
    turns = rest * (1.0 / period)
    v = turns * turns
    return horner(v, COS_TERMS), horner(v, SIN_TERMS) * turns


def places():
    cable = lax.axis_index("cable")
    z = cable // PLANE
    y = (cable // X) % Y
    x = cable % X
    return z, y, x


def cable_id(z, y, x):
    return {"cable": (z * Y + y) * X + x}


def offset_of(step):
    return 2 - step + 3 * (step // 2) - 2 * (step // 3)


def chunk_rows(q):
    return 2 * BLOCKS * sum(CHUNK_BINS[:q]), 2 * BLOCKS * CHUNK_BINS[q]


def steering(group, first_bin, table):
    period = float(50 * NT)
    k = lax.broadcasted_iota(jnp.int32, (8, 128), 0).astype(jnp.float32)
    s = lax.broadcasted_iota(jnp.int32, (8, 128), 1).astype(jnp.float32)
    factor = SUB_LEN ** -0.5
    state = []
    for u in range(WIDE):
        bs = s * (first_bin + group * WIDE + u).astype(jnp.float32)
        cos0, sin0 = unit_circle(bs * k, period)
        cos8, sin8 = unit_circle(bs * 8.0, period)
        cos0, sin0 = cos0 * factor, sin0 * factor
        state.append((cos0, sin0, cos0 * cos8 - sin0 * sin8, sin0 * cos8 + cos0 * sin8, cos8 + cos8))
    for step in range(STRIDE // 16):
        rows = pl.ds(step * 16, 16)
        for u in range(WIDE):
            cos0, sin0, cos1, sin1, twice = state[u]
            table[group * WIDE + u, rows, 0:128] = jnp.concatenate([cos0, cos1], axis=0).astype(jnp.bfloat16)
            table[group * WIDE + u, rows, 128:256] = jnp.concatenate([sin0, sin1], axis=0).astype(jnp.bfloat16)
            cos0, sin0 = twice * cos1 - cos0, twice * sin1 - sin0
            cos1, sin1 = twice * cos0 - cos1, twice * sin0 - sin1
            state[u] = cos0, sin0, cos1, sin1, twice


def widen(q, gathered, wide):
    base, count = chunk_rows(q)
    size = count // BLOCKS
    wide[0:size] = jnp.zeros((size, 128), jnp.float32)
    wide[(LOCAL + 1) * PER:(LOCAL + 1) * PER + size] = jnp.zeros((size, 128), jnp.float32)

    def one(device, carry):
        for b in range(BLOCKS):
            source = pl.multiple_of(device * SHARD + base + b * size, 64)
            target = pl.multiple_of((device * BLOCKS + b + 1) * PER, 8)
            wide[pl.ds(target, size)] = gathered[pl.ds(source, size)].astype(jnp.float32)
        return carry

    lax.fori_loop(0, PLANE, one, 0)


def stack_tile(q, tile, first_bin, wide, table, plus, minus, beams):
    bins = CHUNK_BINS[q]
    before = sum(CHUNK_BINS[:q])
    for f0 in range(8):
        at = tile * 8 + f0
        parts = [wide[pl.ds(c * bins + at, PAD_ROWS, stride=PER), :] for c in range(2)]
        frames = jnp.concatenate(parts, axis=0).astype(jnp.bfloat16)
        out = jnp.dot(frames, table[before + at], preferred_element_type=jnp.float32)
        a_re, b_re = out[:PAD_ROWS, :128], out[:PAD_ROWS, 128:]
        a_im, b_im = out[PAD_ROWS:, :128], out[PAD_ROWS:, 128:]
        plus[pl.ds(f0, PAD_ROWS, stride=STEP), :] = a_re + b_im
        plus[pl.ds(8 + f0, PAD_ROWS, stride=STEP), :] = a_im - b_re
        minus[pl.ds(f0, PAD_ROWS, stride=STEP), :] = a_re - b_im
        minus[pl.ds(8 + f0, PAD_ROWS, stride=STEP), :] = a_im + b_re
    bin_of = first_bin + before + tile * 8 + lax.broadcasted_iota(jnp.int32, (8, 128), 0)
    s = lax.broadcasted_iota(jnp.int32, (8, 128), 1)
    turn_re, turn_im = unit_circle((bin_of * s * STRIDE).astype(jnp.float32), float(50 * NT))
    rows = pl.ds(pl.multiple_of((before // 8 + tile) * 16, 16), 16)
    for side, stacked in enumerate((plus, minus)):
        im_part = turn_im if side == 0 else -turn_im
        re, im = stacked[0:8, :], stacked[8:16, :]
        for r in range(ROWS):
            at = (r + 1) * STEP
            next_re, next_im = stacked[at:at + 8, :], stacked[at + 8:at + 16, :]
            both = [re + (turn_re * next_re + im_part * next_im), im + (turn_re * next_im - im_part * next_re)]
            beams[r, rows, side * 128:(side + 1) * 128] = jnp.concatenate(both, axis=0).astype(jnp.bfloat16)
            re, im = next_re, next_im


def table_row(ref, r, *at):
    return jnp.broadcast_to(ref[at + (pl.ds(r, 1), slice(None))], (8, N))


def hat_of(m, r, slowness, tabs):
    def packed(value):
        return jnp.concatenate([value, value], axis=0).astype(jnp.bfloat16)

    bin_row, weight = table_row(tabs, r, m, 0), table_row(tabs, r, m, 1) * (1.0 / WSTEPS)
    lower, upper = packed(bin_row - float(HALF)), packed(bin_row - float(HALF - 1))
    low_part, high_part, none = packed(1.0 - weight), packed(weight), jnp.zeros((16, N), jnp.bfloat16)
    tiles = []
    for q in range(16):
        at = slowness[q * 16:(q + 1) * 16, :]
        at = jnp.concatenate([at, at], axis=1)
        tiles.append(jnp.where(at == lower, low_part, jnp.where(at == upper, high_part, none)))
    return jnp.concatenate(tiles, axis=0)


def prepare_one(m, r, slot, first_bin, slowness, tabs, hats, starts):
    hats[slot, r] = hat_of(m, r, slowness, tabs)
    bins = (first_bin + lax.broadcasted_iota(jnp.int32, (8, N), 0)).astype(jnp.float32)
    cos0, sin0 = unit_circle(table_row(tabs, r, m, 2) * bins, float(NT))
    starts[m, r, 0:8] = cos0
    starts[m, r, 8:16] = sin0


def project_one(m, r, hat, beams, starts, eighth, total):
    value = jnp.dot(beams[r], hat, preferred_element_type=jnp.float32)
    cos0, sin0 = starts[m, r, 0:8], starts[m, r, 8:16]
    cos8, sin8 = table_row(eighth, r, 0), table_row(eighth, r, 1)
    cos1, sin1 = cos0 * cos8 - sin0 * sin8, sin0 * cos8 + cos0 * sin8
    twice = cos8 + cos8
    for t in range(FT):
        re, im = value[t * 16:t * 16 + 8], value[t * 16 + 8:t * 16 + 16]
        total[t * 16:t * 16 + 8, :] += re * cos0 - im * sin0
        total[t * 16 + 8:t * 16 + 16, :] += re * sin0 + im * cos0
        cos0, sin0, cos1, sin1 = cos1, sin1, twice * cos1 - cos0, twice * sin1 - sin0


def kernel(spectra, slow_bins, weight_steps, delays, slowness, node_spectra, power,
           gathered, table, wide, plus, minus, beams, hats, starts, outgoing, incoming, tabs, eighth, total, sent, landed,
           mine, theirs, finished,
           ag_send, ag_recv, tab_send, tab_recv, sum_send, sum_recv, pow_send, pow_recv, out_sem, raw, raw_sem):
    z, y, x = places()
    freq = lax.axis_index("freq")
    first_bin = BIN0 + freq * F
    reading = [pltpu.make_async_copy(source, raw.at[i], raw_sem.at[i])
               for i, source in enumerate((slow_bins, weight_steps, delays))]
    for copy in reading:
        copy.start()
    barrier = pltpu.get_barrier_semaphore()
    greet = [cable_id(z, y, (x + 1) % X), cable_id(z, y, (x + X - 1) % X),
             cable_id(z, (y + 1) % Y, x), cable_id(z, (y + Y - 1) % Y, x),
             cable_id(z, y, (x + 2) % X), cable_id(z, (y + 2) % Y, x)]
    greet += [cable_id((z + i) % Z, y, x) for i in range(1, Z)]
    greet += [{"freq": (freq + i) % FREQ_DEV} for i in range(1, FREQ_DEV)]
    for device in greet:
        pl.semaphore_signal(barrier, inc=1, device_id=device, device_id_type=MESH)

    own = y * X + x
    for b in range(BLOCKS):
        for c in range(2):
            block = spectra[c, b * STRIDE:(b + 1) * STRIDE, :].astype(jnp.float32).T.astype(jnp.bfloat16)
            for q, bins in enumerate(CHUNK_BINS):
                before = sum(CHUNK_BINS[:q])
                rows = pl.multiple_of(own * SHARD + chunk_rows(q)[0] + (b * 2 + c) * bins, 32)
                gathered[pl.ds(rows, bins), :] = block[before:before + bins]
    pl.semaphore_wait(barrier, len(greet))

    def shifted(way, dx, dy):
        if way == 0:
            return (y + Y + dy) % Y, (x + X + dx) % X
        return (y + Y + dx) % Y, (x + X + dy) % X

    started = []
    by_kind = (1, -1, 2)

    def transfer(q, way, stage, kind, owner):
        base, count = chunk_rows(q)
        start, size = base + way * (count // 2), count // 2
        if stage == 0:
            to = shifted(way, by_kind[kind], 0)
        elif q == CHUNKS - 1:
            to = shifted(way, 0, by_kind[kind])
        else:
            to = shifted(way, 0, by_kind[kind % 2])
            if kind >= 2:
                size = count // 4
                start += size * (kind - 2)
        piece = gathered.at[pl.ds(pl.multiple_of((owner[0] * X + owner[1]) * SHARD + start, 16), size), :]
        return pltpu.make_async_remote_copy(
            src_ref=piece, dst_ref=piece,
            send_sem=ag_send.at[q, way, stage, kind], recv_sem=ag_recv.at[q, way, stage, kind],
            device_id=cable_id(z, *to), device_id_type=MESH)

    def send(q, way, stage, kind, owner):
        copy = transfer(q, way, stage, kind, owner)
        copy.start()
        started.append(copy)

    def arrive(q, way, stage, kind, owner):
        transfer(q, way, stage, kind, owner).wait_recv()

    first = (0, -1, 1, 2)

    def send_own(q):
        for way in range(2):
            for kind in range(3):
                send(q, way, 0, kind, shifted(way, 0, 0))
        for way in range(2):
            for kind in range(3 if q == CHUNKS - 1 else 2):
                send(q, way, 1, kind, shifted(way, 0, 0))

    def from_first_axis(q, j):
        for way in range(2):
            owner = shifted(way, first[j], 0)
            arrive(q, way, 0, j - 1, owner)
            for kind in range(3 if q == CHUNKS - 1 else 2):
                send(q, way, 1 + j, kind, owner)

    def pass_on(q, j):
        for way in range(2):
            for kind, by in ((0, -1), (1, 1)):
                owner = shifted(way, first[j], by)
                arrive(q, way, 1 + j, kind, owner)
                send(q, way, 1 + j, 2 + kind, owner)

    def last_pieces(q):
        for j in range(4):
            for way in range(2):
                owner = shifted(way, first[j], 2)
                arrive(q, way, 1 + j, 2, owner)
                if q == CHUNKS - 1:
                    arrive(q, way, 1 + j, 0, shifted(way, first[j], -1))
                    arrive(q, way, 1 + j, 1, shifted(way, first[j], 1))
                else:
                    arrive(q, way, 1 + j, 3, owner)

    def steer(part, parts):
        def one(group, carry):
            steering(group, first_bin, table)
            return carry

        lax.fori_loop(part * (F // WIDE) // parts, (part + 1) * (F // WIDE) // parts, one, 0)

    def tables_from(i):
        source = (z + Z - i) % Z
        if i == 0:
            incoming[z] = outgoing[z]
        else:
            pltpu.make_async_remote_copy(
                src_ref=outgoing.at[z], dst_ref=incoming.at[source],
                send_sem=tab_send.at[i - 1], recv_sem=tab_recv.at[i - 1],
                device_id=cable_id((z + i) % Z, y, x), device_id_type=MESH).wait_recv()
        for k in range(3):
            tabs[source, k] = incoming[source, k].astype(jnp.float32)[:PAD_ROWS]

    def prepare(m, slot):
        def one(g, carry):
            for j in range(GROUP):
                prepare_one(m, g * GROUP + j, slot, first_bin, slowness, tabs, hats, starts)
            return carry

        lax.fori_loop(0, ROWS // GROUP, one, 0)

    def stack(q, begin, end):
        def four_tiles(group, carry):
            for u in range(4):
                stack_tile(q, group * 4 + u, first_bin, wide, table, plus, minus, beams)
            return carry

        lax.fori_loop(begin // 4, end // 4, four_tiles, 0)

    send_own(0)
    for i, copy in enumerate(reading):
        copy.wait()
        for to in range(Z):
            if to == 0:
                head = jnp.full((1, N), -2000 if i == 0 else 0, jnp.int32)
                rows = jnp.concatenate([head, raw[i, 0:LOCAL, :]], axis=0)
            else:
                rows = raw[i, to * LOCAL - 1:(to + 1) * LOCAL, :]
            rows = jnp.concatenate([rows, jnp.zeros((TAB_ROWS - ROWS, N), jnp.int32)], axis=0)
            outgoing[to, i] = rows.astype(jnp.int16)
    tab_copies = []
    for i in (1, 3, 2):
        copy = pltpu.make_async_remote_copy(
            src_ref=outgoing.at[(z + i) % Z], dst_ref=incoming.at[z],
            send_sem=tab_send.at[i - 1], recv_sem=tab_recv.at[i - 1],
            device_id=cable_id((z + i) % Z, y, x), device_id_type=MESH)
        copy.start()
        tab_copies.append(copy)
    steer(0, 4)
    steer(1, 4)
    from_first_axis(0, 1)
    from_first_axis(0, 2)
    steer(2, 4)
    from_first_axis(0, 3)
    pass_on(0, 0)
    send_own(1)
    steer(3, 4)
    tables_from(0)
    pass_on(0, 1)
    prepare(z, 3)
    pass_on(0, 2)
    pass_on(0, 3)
    from_first_axis(1, 1)
    from_first_axis(1, 2)
    from_first_axis(1, 3)
    for step in (2, 1, 0):
        tables_from(Z - offset_of(step))
        prepare((z + offset_of(step)) % Z, step)
    last_pieces(0)
    widen(0, gathered, wide)
    stack(0, 0, CHUNK_BINS[0] // 8)
    last_pieces(1)
    widen(1, gathered, wide)
    stack(1, 0, CHUNK_BINS[1] // 8)

    def sum_copy(step, m):
        return pltpu.make_async_remote_copy(
            src_ref=sent.at[step], dst_ref=landed.at[step],
            send_sem=sum_send.at[step], recv_sem=sum_recv.at[step],
            device_id=cable_id(m, y, x), device_id_type=MESH)

    def one_step(step, carry):
        m = (z + offset_of(step)) % Z
        cos8, sin8 = unit_circle(tabs[m, 2] * 8.0, float(NT))
        eighth[0] = cos8
        eighth[1] = sin8
        total[...] = jnp.zeros_like(total)
        for r in range(ROWS):
            project_one(m, r, hats[step, r], beams, starts, eighth, total)

        @pl.when(step < Z - 1)
        def _():
            sent[step] = total[...].astype(jnp.bfloat16)
            sum_copy(step, m).start()

        return carry

    lax.fori_loop(0, Z, one_step, 0)
    sums = [sum_copy(step, (z + offset_of(step)) % Z) for step in range(Z - 1)]
    for copy in sums:
        copy.wait_recv()
    others = (landed[0].astype(jnp.float32) + landed[1].astype(jnp.float32)) + landed[2].astype(jnp.float32)
    result = (total[...] + others) * (Z * LOCAL) ** -0.5
    mine[...] = jnp.broadcast_to(jnp.sum(result * result, axis=0, keepdims=True), (8, N))
    power_copies = []
    for i in range(1, FREQ_DEV):
        copy = pltpu.make_async_remote_copy(
            src_ref=mine, dst_ref=theirs.at[i - 1],
            send_sem=pow_send.at[i - 1], recv_sem=pow_recv.at[i - 1],
            device_id={"freq": (freq + i) % FREQ_DEV}, device_id_type=MESH)
        copy.start()
        power_copies.append(copy)
    finished[...] = result
    writing = pltpu.make_async_copy(finished, node_spectra, out_sem)
    writing.start()
    for copy in power_copies:
        copy.wait_recv()
    power[...] = (mine[0:1] + theirs[0, 0:1] + theirs[1, 0:1] + theirs[2, 0:1]) * (1.0 / (F * FREQ_DEV))
    for copy in started + tab_copies + sums + power_copies:
        copy.wait_send()
    writing.wait()


def turn_kernel(sums, power_row, node_spectra, power):
    split = sums[...].reshape(FT, 2, 8, N // 2)
    for c in range(2):
        node_spectra[:, c, :] = split[:, c].reshape(F, N // 2).T
    power[...] = power_row[...]


def slowness_rows():
    s = np.full((256, 128), 4000.0, np.float32)
    s[0:HALF + 1] = np.arange(HALF + 1)[:, None]
    s[129:129 + HALF] = -np.arange(1, HALF + 1)[:, None]
    return jnp.asarray(s, jnp.bfloat16)


def shards(spectra, slow_bins, weight_steps, delays):
    vmem = pl.BlockSpec(memory_space=pltpu.VMEM)
    f32, bf16, dma = jnp.float32, jnp.bfloat16, pltpu.SemaphoreType.DMA
    sums, power_row = pl.pallas_call(
        kernel,
        out_shape=(jax.ShapeDtypeStruct((2 * F, N), f32), jax.ShapeDtypeStruct((1, N), f32)),
        in_specs=[vmem] + [pl.BlockSpec(memory_space=pl.ANY)] * 3 + [vmem],
        out_specs=(pl.BlockSpec(memory_space=pl.ANY), vmem),
        scratch_shapes=[
            pltpu.VMEM((PLANE * SHARD, 128), bf16),
            pltpu.VMEM((F, STRIDE, 256), bf16),
            pltpu.VMEM((PAD_ROWS * PER, 128), f32),
            pltpu.VMEM((PAD_ROWS * STEP, 128), f32),
            pltpu.VMEM((PAD_ROWS * STEP, 128), f32),
            pltpu.VMEM((ROWS, 2 * F, 256), bf16),
            pltpu.VMEM((Z, ROWS, 256, N), bf16),
            pltpu.VMEM((Z, ROWS, 16, N), f32),
            pltpu.VMEM((Z, 3, TAB_ROWS, N), jnp.int16),
            pltpu.VMEM((Z, 3, TAB_ROWS, N), jnp.int16),
            pltpu.VMEM((Z, 3, PAD_ROWS, N), f32),
            pltpu.VMEM((2, PAD_ROWS, N), f32),
            pltpu.VMEM((2 * F, N), f32),
            pltpu.VMEM((Z - 1, 2 * F, N), bf16),
            pltpu.VMEM((Z - 1, 2 * F, N), bf16),
            pltpu.VMEM((8, N), f32),
            pltpu.VMEM((FREQ_DEV - 1, 8, N), f32),
            pltpu.VMEM((2 * F, N), f32),
            dma((CHUNKS, 2, 5, 4)),
            dma((CHUNKS, 2, 5, 4)),
            dma((Z - 1,)),
            dma((Z - 1,)),
            dma((Z - 1,)),
            dma((Z - 1,)),
            dma((FREQ_DEV - 1,)),
            dma((FREQ_DEV - 1,)),
            dma,
            pltpu.VMEM((3, Z * LOCAL, N), jnp.int32),
            dma((3,)),
        ],
        compiler_params=pltpu.CompilerParams(
            collective_id=0, has_side_effects=True, vmem_limit_bytes=63 * 1024 * 1024
        ),
    )(spectra, slow_bins, weight_steps, delays, slowness_rows())
    node_spectra, power = pl.pallas_call(
        turn_kernel,
        out_shape=(jax.ShapeDtypeStruct((N, 2, F), f32), jax.ShapeDtypeStruct((1, N), f32)),
        grid=(2,),
        in_specs=[pl.BlockSpec((2 * F, N // 2), lambda i: (0, i)), pl.BlockSpec((1, N // 2), lambda i: (0, i))],
        out_specs=(pl.BlockSpec((N // 2, 2, F), lambda i: (i, 0, 0)), pl.BlockSpec((1, N // 2), lambda i: (0, i))),
    )(sums, power_row)
    return node_spectra, power.reshape(N)


def solution(mesh):
    placed = (P(None, "cable", "freq"), P(None, "cable"), P(None, "cable"), P(None, "cable"))
    return jax.shard_map(
        shards,
        mesh=mesh,
        in_specs=placed,
        out_specs=(P("cable", None, "freq"), P("cable")),
        check_vma=False,
    )
```
